32 devices in a mesh: space: 8 (over z, y), dir: 4 (over x, core).
Axes of the slice: x: 2, y: 2, z: 4, core: 2. Of those that a mesh axis runs over, the one named last changes fastest.
Arguments:
- state: float32 [36, 32, 128, 256], P('dir', None, 'space'), may hold values from -6 to 6
- target: float32 [36, 32, 128, 256], P('dir', None, 'space'), may hold values from -6 to 6
- w_in: bfloat16 [36, 32, 256], P('dir'), may hold values from -0.1875 to 0.1875
- w_out: bfloat16 [256, 36, 32], P(None, 'dir'), may hold values from -0.375 to 0.375
- sea_mask: int32 [128, 256], P('space'), may hold values from 0 to 1
- sea_count: int32 [128], P('space'), may hold values from 1 to 256, as said below
- turn_sign: int32 [128, 256], P('space'), may hold values from -1 to 1, as said below
Outputs:
- next_state: float32 [36, 32, 128, 256], P('dir', None, 'space')
- grad_in: float32 [36, 32, 256], P('dir')
- grad_out: float32 [256, 36, 32], P(None, 'dir')
The draws below stay inside these ranges and needn't reach their ends.
Inputs may be any that keep to these rules, and one draw needn't show every extreme that they name: sea_count holds, for each row, the number of ones of sea_mask in that row. turn_sign is -1 or +1.
All inputs are finite; a program needn't handle non-finite values.
Results may differ from the reference program's by a relative error of at most 0.003.
Values may be sent and summed in bfloat16 or wider, within the bound.
No kernel may reach another device: no remote copies, remote signals or barrier semaphores. Data moves between devices by JAX's collectives and lax.ppermute only.
A program may use at most 128 MiB of HBM per device.

```python
import math
import jax
import jax.numpy as jnp
from jax import lax

NDIR = 36
NFREQ = 32
HIDDEN_SIZE = 256
ROWS_DEV = 16
NLON = 256
NLAT = 128
N_DIR = 4


def sea_layout(key):
    rows = jnp.arange(NLAT, dtype=jnp.int32)
    level = 300 + 650 * rows // max(NLAT - 1, 1)
    draws = jax.random.randint(key, (NLAT, NLON), 0, 1000)
    keeper = jax.random.randint(jax.random.fold_in(key, 7), (NLAT,), 0, NLON)
    columns = jnp.arange(NLON, dtype=jnp.int32)
    kept = columns[None, :] == keeper[:, None]
    sea = (draws < level[:, None]) & (rows[:, None] > 0) | kept | (rows[:, None] == NLAT - 1)
    return sea.astype(jnp.int32)


def draw_sea_mask(key, part):
    return sea_layout(key)


def draw_sea_count(key, part):
    return jnp.sum(sea_layout(key), axis=1).astype(jnp.int32)


def draw_turn_sign(key, part):
    key = jax.random.fold_in(key, 11)
    return (jax.random.randint(key, (NLAT, NLON), 0, 2) * 2 - 1).astype(jnp.int32)


def block_levels(own_key, dims, split, least, high):
    def one(position, blocks):
        heights = jax.random.uniform(jax.random.fold_in(jax.random.fold_in(own_key, 6), position), (blocks,), jnp.float32, least / len(split), high / len(split))
        return jnp.repeat(jnp.exp(heights), dims[position] // blocks).reshape((-1,) + (1,) * (len(dims) - position - 1))

    gain = one(*split[0])
    for cut in split[1:]:
        gain = gain * one(*cut)
    return gain


def centred(rng, shape, deviation, most, shards=(), kind=jnp.bfloat16):
    drawn = jax.random.normal(rng, shape, jnp.float32) * deviation
    if len(shards) > 0:
        drawn = block_levels(rng, shape, shards, -0.22, 0.18) * drawn
    return jnp.clip(drawn, min=-most, max=most).astype(kind)


def setup_inputs(seed: int = 0) -> dict:
    key_of = jax.random.split(jax.random.key(seed), 8)
    state = centred(key_of[0], (NDIR, NFREQ, NLAT, NLON), 1.0, 6.0, ((0, 4), (2, 8)), jnp.float32)
    target = centred(key_of[1], (NDIR, NFREQ, NLAT, NLON), 1.0, 6.0, ((0, 4), (2, 8)), jnp.float32)
    w_in = centred(key_of[2], (NDIR, NFREQ, HIDDEN_SIZE), (NDIR * NFREQ) ** -0.5, 0.1875, ((0, 4),))
    w_out = centred(key_of[3], (HIDDEN_SIZE, NDIR, NFREQ), HIDDEN_SIZE ** -0.5, 0.375, ((1, 4),))
    sea_mask = draw_sea_mask(jax.random.fold_in(key_of[7], 71), 0)
    sea_count = draw_sea_count(jax.random.fold_in(key_of[7], 71), 0)
    turn_sign = draw_turn_sign(jax.random.fold_in(key_of[7], 71), 0)
    return dict(state=state, target=target, w_in=w_in, w_out=w_out, sea_mask=sea_mask, sea_count=sea_count, turn_sign=turn_sign)


def courant():
    angle = 2.0 * math.pi * (jnp.arange(NDIR, dtype=jnp.float32) + 0.5) / NDIR
    speed = 1.0 / (1.0 + 2.3 * jnp.arange(NFREQ, dtype=jnp.float32) / NFREQ)
    cx = 0.4 * jnp.cos(angle)[:, None] * speed[None, :]
    cy = 0.4 * jnp.sin(angle)[:, None] * speed[None, :]
    return cx[:, :, None, None], cy[:, :, None, None]


def sector_sum(parts):
    return jnp.sum(parts, axis=0)


def reference(state, target, w_in, w_out, sea_mask, sea_count, turn_sign):
    maskf = sea_mask.astype(jnp.float32)
    field = state * maskf[None, None]
    cx, cy = courant()
    circled = jnp.concatenate([field[-1:], field, field[:1]], axis=0)
    padded = jnp.pad(circled, ((0, 0), (0, 0), (1, 1), (1, 1)))
    w_in_s = w_in.astype(jnp.float32).reshape(N_DIR, NDIR // N_DIR, NFREQ, HIDDEN_SIZE)
    w_out_s = w_out.astype(jnp.float32).reshape(HIDDEN_SIZE, N_DIR, NDIR // N_DIR, NFREQ)
    blocks = NLAT // ROWS_DEV

    def block(carry, index):
        g_in, g_out = carry
        start = (index * ROWS_DEV).astype(jnp.int32)
        window = lax.dynamic_slice_in_dim(padded, start, ROWS_DEV + 2, 2)
        mask_b = lax.dynamic_slice_in_dim(maskf, start, ROWS_DEV, 0)
        count_b = lax.dynamic_slice_in_dim(sea_count, start, ROWS_DEV, 0).astype(jnp.float32)
        sign_b = lax.dynamic_slice_in_dim(turn_sign, start, ROWS_DEV, 0)
        tgt_b = lax.dynamic_slice_in_dim(target, start, ROWS_DEV, 2)
        centre = window[1:-1, :, 1:-1, 1:-1]
        west = window[1:-1, :, 1:-1, :-2]
        east = window[1:-1, :, 1:-1, 2:]
        south = window[1:-1, :, :-2, 1:-1]
        north = window[1:-1, :, 2:, 1:-1]
        advect = -(jnp.maximum(cx, 0.0) * (centre - west) + jnp.minimum(cx, 0.0) * (east - centre))
        advect = advect - (jnp.maximum(cy, 0.0) * (centre - south) + jnp.minimum(cy, 0.0) * (north - centre))
        upstream = jnp.where((sign_b > 0)[None, None], window[:-2, :, 1:-1, 1:-1], window[2:, :, 1:-1, 1:-1])
        turning = -0.3 * (centre - upstream)
        spec_in = centre.astype(jnp.bfloat16)
        spec_s = spec_in.astype(jnp.float32).reshape(N_DIR, NDIR // N_DIR, NFREQ, ROWS_DEV, NLON)
        pre = sector_sum(jnp.einsum('sdfyx,sdfh->shyx', spec_s, w_in_s))
        hidden = jax.nn.silu(pre).astype(jnp.bfloat16)
        hid32 = hidden.astype(jnp.float32)
        source = jnp.einsum('hyx,hdf->dfyx', hid32, w_out.astype(jnp.float32))
        new = mask_b[None, None] * (centre + advect + turning + 0.5 * source)
        weight = (1.0 / count_b)[:, None] * mask_b
        back_src = (1.0 * weight[None, None] * (new - tgt_b)).astype(jnp.bfloat16)
        back32 = back_src.astype(jnp.float32)
        g_out = g_out + jnp.einsum('hyx,dfyx->hdf', hid32, back32)
        back_s = back32.reshape(N_DIR, NDIR // N_DIR, NFREQ, ROWS_DEV, NLON)
        back_hidden = sector_sum(jnp.einsum('hsdf,sdfyx->shyx', w_out_s, back_s))
        sig = jax.nn.sigmoid(pre)
        back_pre = (back_hidden * sig * (1.0 + pre * (1.0 - sig))).astype(jnp.bfloat16)
        g_in = g_in + jnp.einsum('dfyx,hyx->dfh', spec_in.astype(jnp.float32), back_pre.astype(jnp.float32))
        return (g_in, g_out), new

    init = (jnp.zeros((NDIR, NFREQ, HIDDEN_SIZE), jnp.float32), jnp.zeros((HIDDEN_SIZE, NDIR, NFREQ), jnp.float32))
    (grad_in, grad_out), pieces = lax.scan(block, init, jnp.arange(blocks, dtype=jnp.int32))
    next_state = jnp.moveaxis(pieces, 0, 2).reshape(NDIR, NFREQ, NLAT, NLON)
    return next_state, grad_in, grad_out
```

```python
import math

import jax
import jax.numpy as jnp
from jax import lax
from jax.experimental import pallas as pl
from jax.experimental.pallas import tpu as pltpu
from jax.sharding import PartitionSpec as P

NDIR = 36
ROWS = 8
LANES = 128
PRE_SCALE = 64.0
BACK_SCALE = 2.0**-8

BF16, F16, F32 = jnp.bfloat16, jnp.float16, jnp.float32


def swap(value, axis, bit):
    count = lax.axis_size(axis)
    return lax.ppermute(value, axis, [(i, i ^ bit) for i in range(count)])


def call(body, grid, ins, outs, cost, aliases=None, name=None):
    return pl.pallas_call(
        body,
        grid=grid,
        in_specs=[spec for _, spec in ins],
        out_specs=[spec for _, spec in outs],
        out_shape=[shape for shape, _ in outs],
        input_output_aliases=aliases or {},
        compiler_params=pltpu.CompilerParams(vmem_limit_bytes=40 << 20),
        cost_estimate=pl.CostEstimate(flops=cost[0], bytes_accessed=cost[1], transcendentals=0),
        name=name,
    )(*[value for value, _ in ins])


def shape(dims, dtype):
    return jax.ShapeDtypeStruct(dims, dtype)


def first_row(core, side, half):
    return core * half if side == 0 else (1 - core) * half


def encode_body(core_ref, state_ref, mask_ref, w_ref, spec_ref, own_ref, send_ref):
    core = core_ref[0]
    bins, rows, lanes = state_ref.shape
    flat = state_ref.reshape(bins * rows, lanes)
    half = rows // 2
    for side, out in ((0, own_ref), (1, send_ref)):
        first = first_row(core, side, half)
        cols = []
        for i in range(half):
            row = flat[pl.ds(first + i, bins, stride=rows), :]
            cols.append((row * mask_ref[pl.ds(first + i, 1), :]).astype(BF16))
        field = jnp.concatenate(cols, axis=1)
        spec_ref[:, side * half * lanes : (side + 1) * half * lanes] = field
        out[...] = lax.dot_general(
            w_ref[...], field, (((0,), (0,)), ((), ())), preferred_element_type=F32
        )


def encode(core, state, mask, w_in, chunk):
    bins, rows, lon = state.shape
    hidden = w_in.shape[1]
    parts = lon // LANES
    wide = ROWS * LANES
    return call(
        encode_body,
        (parts,),
        [
            (core, pl.BlockSpec(memory_space=pltpu.SMEM)),
            (state, pl.BlockSpec((bins, ROWS, LANES), lambda j: (0, chunk, j))),
            (mask, pl.BlockSpec((ROWS, LANES), lambda j: (chunk, j))),
            (w_in, pl.BlockSpec((bins, hidden), lambda j: (0, 0))),
        ],
        [
            (shape((bins, parts * wide), BF16), pl.BlockSpec((bins, wide), lambda j: (0, j))),
            (shape((hidden, parts * wide // 2), F32), pl.BlockSpec((hidden, wide // 2), lambda j: (0, j))),
            (shape((hidden, parts * wide // 2), F32), pl.BlockSpec((hidden, wide // 2), lambda j: (0, j))),
        ],
        (2 * bins * hidden * parts * wide, 4 * bins * parts * wide + 8 * hidden * parts * wide),
        name="encode",
    )


def stencil_body(coef_ref, state_ref, low_ref, high_ref, edge_ref, mask_ref, sign_ref, base_ref):
    d = pl.program_id(0)
    ndir = pl.num_programs(0)
    nfreq, rows, lon = base_ref.shape
    mask = mask_ref[...]
    ahead = sign_ref[...] > 0
    lane = lax.broadcasted_iota(jnp.int32, (rows, lon), 1)
    row = lax.broadcasted_iota(jnp.int32, (rows, lon), 0)

    def sector(below, above):
        def one(f, _):
            b = d * nfreq + f
            here = state_ref[b]
            field = here * mask
            west = jnp.where(lane == 0, 0.0, pltpu.roll(field, 1, 1))
            east = jnp.where(lane == lon - 1, 0.0, pltpu.roll(field, lon - 1, 1))
            edge = edge_ref[pl.ds(b, 1), :]
            south = jnp.where(row == 0, edge, pltpu.roll(field, 1, 0))
            north = jnp.where(row == rows - 1, edge, pltpu.roll(field, rows - 1, 0))
            upstream = jnp.where(ahead, below(b, f), above(b, f))
            total = coef_ref[0, b] * here + coef_ref[1, b] * west + coef_ref[2, b] * east
            total = total + coef_ref[3, b] * south + coef_ref[4, b] * north + 0.3 * upstream
            base_ref[f] = total * mask
            return 0

        lax.fori_loop(0, nfreq, one, 0, unroll=4)

    def inside_low(b, f):
        return state_ref[b - nfreq]

    def inside_high(b, f):
        return state_ref[b + nfreq]

    @pl.when(d == 0)
    def _():
        sector(lambda b, f: low_ref[f], inside_high)

    @pl.when(d == ndir - 1)
    def _():
        sector(inside_low, lambda b, f: high_ref[f])

    @pl.when(jnp.logical_and(d > 0, d < ndir - 1))
    def _():
        sector(inside_low, inside_high)


def stencil(coef, state, low, high, edge, mask, sign, ndir):
    bins, rows, lon = state.shape
    nfreq = bins // ndir

    def whole(value):
        return (value, pl.BlockSpec(value.shape, lambda d: (0,) * value.ndim))

    return call(
        stencil_body,
        (ndir,),
        [(coef, pl.BlockSpec(memory_space=pltpu.SMEM))]
        + [whole(v) for v in (state, low, high, edge, mask, sign)],
        [(shape(state.shape, F32), pl.BlockSpec((nfreq, rows, lon), lambda d: (d, 0, 0)))],
        (20 * state.size, 8 * state.size),
        name="stencil",
    )[0]


def decode_body(
    core_ref, own_ref, other_ref, w_ref, base_ref, target_ref, mask_ref, weight_ref, seed_ref,
    next_ref, grad_ref, back_own_ref, back_send_ref, back_scr,
):
    core = core_ref[0]
    bins, rows, lanes = base_ref.shape
    base = base_ref.reshape(bins * rows, lanes)
    target = target_ref.reshape(bins * rows, lanes)
    result = next_ref.reshape(bins * rows, lanes)
    half = rows // 2

    @pl.when(pl.program_id(0) == 0)
    def _():
        grad_ref[...] = seed_ref[...]

    for side, hid_ref, out in ((0, own_ref, back_own_ref), (1, other_ref, back_send_ref)):
        first = first_row(core, side, half)
        hid = hid_ref[...]
        source = lax.dot_general(w_ref[...], hid, (((0,), (0,)), ((), ())), preferred_element_type=F32)
        for i in range(half):
            y = first + i
            at = pl.ds(y, bins, stride=rows)
            part = source[:, i * lanes : (i + 1) * lanes]
            new = base[at, :] + (0.5 * mask_ref[pl.ds(y, 1), :]) * part
            result[at, :] = new
            back = (weight_ref[pl.ds(y, 1), :] * (new - target[at, :])).astype(BF16)
            back_scr[:, i * lanes : (i + 1) * lanes] = back
        back = back_scr[...]
        grad_ref[...] += lax.dot_general(hid, back, (((1,), (1,)), ((), ())), preferred_element_type=F32)
        out[...] = jnp.dot(w_ref[...], back, preferred_element_type=F32)


def decode(core, own, other, w_out, base, target, mask, weight, seed, chunk):
    bins, rows, lon = base.shape
    hidden = w_out.shape[0]
    parts = lon // LANES
    wide = ROWS * LANES // 2
    cells = pl.BlockSpec((bins, ROWS, LANES), lambda j: (0, chunk, j))
    units = pl.BlockSpec((hidden, wide), lambda j: (0, j))
    plane = pl.BlockSpec((ROWS, LANES), lambda j: (chunk, j))
    fixed = pl.BlockSpec((hidden, bins), lambda j: (0, 0))
    return pl.pallas_call(
        decode_body,
        grid=(parts,),
        in_specs=[pl.BlockSpec(memory_space=pltpu.SMEM), units, units, fixed, cells, cells, plane, plane, fixed],
        out_specs=[cells, fixed, units, units],
        out_shape=[
            shape(base.shape, F32),
            shape((hidden, bins), F32),
            shape((hidden, parts * wide), F32),
            shape((hidden, parts * wide), F32),
        ],
        scratch_shapes=[pltpu.VMEM((bins, wide), BF16)],
        input_output_aliases={4: 0},
        compiler_params=pltpu.CompilerParams(vmem_limit_bytes=40 << 20),
        cost_estimate=pl.CostEstimate(
            flops=12 * bins * hidden * parts * wide,
            bytes_accessed=24 * bins * parts * wide + 12 * hidden * parts * wide,
            transcendentals=0,
        ),
        name="decode",
    )(core, own, other, w_out, base, target, mask, weight, seed)


def collect_body(spec_ref, own_ref, other_ref, seed_ref, grad_ref):
    @pl.when(pl.program_id(0) == 0)
    def _():
        grad_ref[...] = seed_ref[...]

    back = jnp.concatenate([own_ref[...], other_ref[...]], axis=1)
    grad_ref[...] += lax.dot_general(
        spec_ref[...], back, (((1,), (1,)), ((), ())), preferred_element_type=F32
    )


def collect(spec, own, other, seed):
    bins, cells = spec.shape
    hidden = own.shape[0]
    wide = ROWS * LANES
    units = pl.BlockSpec((hidden, wide // 2), lambda j: (0, j))
    fixed = pl.BlockSpec((bins, hidden), lambda j: (0, 0))
    return call(
        collect_body,
        (cells // wide,),
        [(spec, pl.BlockSpec((bins, wide), lambda j: (0, j))), (own, units), (other, units), (seed, fixed)],
        [(shape((bins, hidden), F32), fixed)],
        (2 * bins * hidden * cells, 2 * bins * cells + 2 * hidden * cells),
        name="collect",
    )[0]


def space_sum(value):
    n = value.shape[0]
    extra = 16

    def packed(total, power):
        scaled = (total * jnp.exp2(-power)).astype(F16)
        return jnp.concatenate(
            [scaled, jnp.broadcast_to(power.astype(F16), (extra, value.shape[1]))], axis=0
        )

    def opened(sent):
        power = sent[n : n + 1].astype(F32)
        return (sent[:n].astype(F32) * jnp.exp2(power), power)

    most = jnp.maximum(jnp.max(jnp.abs(value)), 2.0**-100)
    power = jnp.full((1, value.shape[1]), jnp.ceil(jnp.log2(most)), F32)
    total = value
    bit = 1
    count = lax.axis_size("space")
    assert count & (count - 1) == 0
    while bit < count:
        mine = packed(total, power)
        other, other_power = opened(swap(mine, "space", bit))
        total, _ = opened(mine)
        total = total + other
        power = jnp.maximum(power, other_power) + 1.0
        bit *= 2
    return total


def courant(first, count, nfreq):
    bins = (first + jnp.arange(count, dtype=jnp.int32)).astype(F32)
    angle = 2.0 * math.pi * (bins + 0.5) / NDIR
    speed = 1.0 / (1.0 + 2.3 * jnp.arange(nfreq, dtype=F32) / nfreq)
    cx = 0.4 * jnp.cos(angle)[:, None] * speed[None, :]
    cy = 0.4 * jnp.sin(angle)[:, None] * speed[None, :]
    return (cx.reshape(-1), cy.reshape(-1))


def on_device(state, target, w_in, w_out, sea_mask, sea_count, turn_sign):
    ndir, nfreq, rows, lon = state.shape
    bins = ndir * nfreq
    hidden = w_in.shape[2]
    place = lax.axis_index("dir")
    sectors = lax.axis_size("dir")
    spaces = lax.axis_size("space")
    assert sectors == 4 and ndir * sectors == NDIR
    core = place % 2
    core_ref = core.reshape(1)
    state = state.reshape(bins, rows, lon)
    target = target.reshape(bins, rows, lon)
    w_in = w_in.reshape(bins, hidden)
    w_out = w_out.reshape(hidden, bins)
    maskf = sea_mask.astype(F32)
    countf = sea_count.astype(F32)
    weight = (1.0 / countf)[:, None] * maskf
    parts = lon // LANES
    chunks = rows // ROWS
    half = ROWS // 2

    north = place >= sectors // 2
    edge = lax.dynamic_index_in_dim(state, jnp.where(north, 0, rows - 1), 1, False)
    edge = edge * lax.dynamic_index_in_dim(maskf, jnp.where(north, 0, rows - 1), 0, True)
    pairs = []
    for s in range(spaces):
        for d in range(sectors):
            to = s - 1 if d >= sectors // 2 else s + 1
            if 0 <= to < spaces:
                pairs.append((s * sectors + d, to * sectors + d))
    last, first = state[bins - nfreq :], state[:nfreq]
    upper = core == 1
    near = swap(jnp.where(upper, first, last).astype(F16), "dir", 1).astype(F32)
    far = swap(jnp.where(upper, last, first).astype(F16), "dir", 3).astype(F32)
    edge = lax.ppermute(edge.astype(F16), ("space", "dir"), pairs).astype(F32)
    low = jnp.where(upper, near, far)
    high = jnp.where(upper, far, near)
    cx, cy = courant(place * ndir, ndir, nfreq)
    coef = jnp.stack(
        [
            1.0 - jnp.abs(cx) - jnp.abs(cy) - 0.3,
            jnp.maximum(cx, 0.0),
            -jnp.minimum(cx, 0.0),
            jnp.maximum(cy, 0.0),
            -jnp.minimum(cy, 0.0),
        ]
    )

    encoded = [encode(core_ref, state, maskf, w_in, c) for c in range(chunks)]
    base = stencil(coef, state, low, high, edge, maskf, turn_sign, ndir)

    pres, hids = [], []
    for c in range(chunks):
        _, own, send = encoded[c]
        chip = ((own + swap(send, "dir", 1)) * PRE_SCALE).astype(F16)
        pre = (chip.astype(F32) + swap(chip, "dir", 2).astype(F32)) * (1.0 / PRE_SCALE)
        pres.append(pre)
        hids.append(jax.nn.silu(pre).astype(BF16))

    grad_out = jnp.zeros((hidden, bins), F32)
    backs = []
    for c in range(chunks):
        other = swap(hids[c], "dir", 1)
        base, grad_out, own, send = decode(
            core_ref, hids[c], other, w_out, base, target, maskf, weight, grad_out, c
        )
        counts = lax.dynamic_slice_in_dim(countf, c * ROWS + core * half, half, 0)
        counts = jnp.tile(jnp.repeat(counts, LANES), parts)[None]
        chip = ((own + swap(send, "dir", 1)) * (counts * BACK_SCALE)).astype(F16)
        backs.append((chip, counts))

    grad_in = jnp.zeros((bins, hidden), F32)
    for c in range(chunks):
        chip, counts = backs[c]
        back = (chip.astype(F32) + swap(chip, "dir", 2).astype(F32)) * ((1.0 / BACK_SCALE) / counts)
        pre = pres[c]
        sig = jax.nn.sigmoid(pre)
        back_pre = (back * sig * (1.0 + pre * (1.0 - sig))).astype(BF16)
        grad_in = collect(encoded[c][0], back_pre, swap(back_pre, "dir", 1), grad_in)

    grad_out = space_sum(grad_out)
    grad_in = space_sum(grad_in)
    return (
        base.reshape(ndir, nfreq, rows, lon),
        grad_in.reshape(ndir, nfreq, hidden),
        grad_out.reshape(hidden, ndir, nfreq),
    )


def solution(mesh):
    in_specs = (
        P("dir", None, "space", None),
        P("dir", None, "space", None),
        P("dir", None, None),
        P(None, "dir", None),
        P("space", None),
        P("space"),
        P("space", None),
    )
    out_specs = (P("dir", None, "space", None), P("dir", None, None), P(None, "dir", None))
    return jax.shard_map(
        on_device, mesh=mesh, in_specs=in_specs, out_specs=out_specs, check_vma=False
    )
```

```python
import math

import jax
import jax.numpy as jnp
import numpy as np
from jax import lax
from jax.experimental import pallas as pl
from jax.experimental.pallas import tpu as pltpu
from jax.sharding import PartitionSpec as P

NDIR = 36
ROWS = 8
LANES = 128
PRE_SCALE = 64.0
BACK_SCALE = 2.0**-8
POWER_ROWS = 16

BF16, F16, F32 = jnp.bfloat16, jnp.float16, jnp.float32
VMEM = pl.BlockSpec(memory_space=pltpu.VMEM)
SMEM = pl.BlockSpec(memory_space=pltpu.SMEM)
HBM = pl.BlockSpec(memory_space=pltpu.HBM)
ANY = pl.BlockSpec(memory_space=pl.ANY)


def swap(value, axis, bit):
    count = lax.axis_size(axis)
    return lax.ppermute(value, axis, [(i, i ^ bit) for i in range(count)])


def call(body, ins, outs, cost, after=(), aliases=None, scratch=(), limit=16, name=None):
    n = len(ins)

    def run(*refs):
        body(*refs[:n], *refs[n + len(after) :])

    return pl.pallas_call(
        run,
        in_specs=[spec for _, spec in ins] + [ANY] * len(after),
        out_specs=[VMEM if len(out) == 2 else out[2] for out in outs],
        out_shape=[jax.ShapeDtypeStruct(*out[:2]) for out in outs],
        scratch_shapes=list(scratch),
        input_output_aliases=aliases or {},
        compiler_params=pltpu.CompilerParams(vmem_limit_bytes=limit << 20),
        cost_estimate=pl.CostEstimate(flops=cost[0], bytes_accessed=cost[1], transcendentals=0),
        name=name,
    )(*[value for value, _ in ins], *after)


def first_row(core, own):
    half = ROWS // 2
    return core * half if own else (1 - core) * half


def pick(ref, core, own, chunk, i, j):
    at = chunk * ROWS + i
    lanes = slice(j * LANES, (j + 1) * LANES)
    low, high = ref[at : at + 1, lanes], ref[at + ROWS // 2 : at + ROWS // 2 + 1, lanes]
    return jnp.where((core == 0) == own, low, high).astype(F32)


def count_of(count_ref, core, own, chunk, i):
    value = count_ref[chunk * ROWS + first_row(core, own) + i]
    return jnp.full((1, LANES), value, jnp.int32).astype(F32)


def encode_rows(place_ref, tiles_ref, mask_ref, w_ref, spec_ref, out_ref, chunk, own):
    parts, bins = tiles_ref.shape[1:3]
    half = ROWS // 2
    wide = half * LANES
    core = place_ref[0] % 2
    first = first_row(core, own)
    for j in range(parts):
        flat = tiles_ref.at[chunk, j].reshape(bins * ROWS, LANES)
        cols = []
        for i in range(half):
            row = flat[pl.ds(first + i, bins, stride=ROWS), :]
            cols.append((row * pick(mask_ref, core, own, chunk, i, j)).astype(BF16))
        field = jnp.concatenate(cols, axis=1)
        spec_ref[:, j * wide : (j + 1) * wide] = field
        out_ref[:, j * wide : (j + 1) * wide] = lax.dot_general(
            w_ref[...], field, (((0,), (0,)), ((), ())), preferred_element_type=F32
        )


def encode_first(place, state, mask, w_in, after=()):
    bins, rows, lon = state.shape
    hidden = w_in.shape[1]
    chunks, parts = rows // ROWS, lon // LANES
    cells = parts * ROWS * LANES // 2

    def body(place_ref, state_ref, mask_ref, w_ref, tiles_ref, spec_ref, out_ref, sems):
        copies = [
            [
                pltpu.make_async_copy(
                    state_ref.at[:, pl.ds(c * ROWS, ROWS), pl.ds(j * LANES, LANES)],
                    tiles_ref.at[c, j],
                    sems.at[c * parts + j],
                )
                for j in range(parts)
            ]
            for c in range(chunks)
        ]
        for row in copies:
            for copy in row:
                copy.start()
        for copy in copies[0]:
            copy.wait()
        encode_rows(place_ref, tiles_ref, mask_ref, w_ref, spec_ref, out_ref, 0, False)
        for row in copies[1:]:
            for copy in row:
                copy.wait()

    return call(
        body,
        [(place, SMEM), (state, HBM), (mask, VMEM), (w_in, VMEM)],
        [((chunks, parts, bins, ROWS, LANES), F32), ((bins, cells), BF16), ((hidden, cells), F32)],
        (2 * bins * hidden * cells, 4 * bins * rows * lon),
        scratch=[pltpu.SemaphoreType.DMA((chunks * parts,))],
        after=after,
        limit=54,
        name="encode_first",
    )


def encode(place, tiles, mask, w_in, chunk, own, after=()):
    parts, bins = tiles.shape[1:3]
    hidden = w_in.shape[1]
    cells = parts * ROWS * LANES // 2

    def body(*refs):
        encode_rows(*refs, chunk, own)

    return call(
        body,
        [(place, SMEM), (tiles, VMEM), (mask, VMEM), (w_in, VMEM)],
        [((bins, cells), BF16), ((hidden, cells), F32)],
        (2 * bins * hidden * cells, 4 * bins * cells),
        after=after,
        name="encode",
    )


def stencil(place, coef, tiles, low, high, edge, mask, sign, count, target, chunk, ndir, after=()):
    chunks, parts, bins = tiles.shape[:3]
    nfreq = bins // ndir
    half = ROWS // 2
    wide = half * LANES

    def body(
        place_ref, coef_ref, tiles_ref, low_ref, high_ref, edge_ref, mask_ref, sign_ref, count_ref, target_ref,
        base_ref, goal_ref, unit_ref, down_ref, up_ref, sems,
    ):
        copies = []
        for j in range(parts):
            copy = pltpu.make_async_copy(
                target_ref.at[:, pl.ds(chunk * ROWS, ROWS), pl.ds(j * LANES, LANES)], goal_ref.at[j], sems.at[j]
            )
            copy.start()
            copies.append(copy)
        place = place_ref[0]
        unit_ref[...] = jnp.full(unit_ref.shape, 1.0 / PRE_SCALE, F32)
        for i in range(half):
            counts = count_of(count_ref, place % 2, False, chunk, i)
            for j in range(parts):
                at = slice(j * wide + i * LANES, j * wide + (i + 1) * LANES)
                down_ref[:, at] = counts * BACK_SCALE
                up_ref[:, at] = (1.0 / BACK_SCALE) / counts
        lane = lax.broadcasted_iota(jnp.int32, (ROWS, LANES), 1)
        row = lax.broadcasted_iota(jnp.int32, (ROWS, LANES), 0)

        def plane(ref, c, j):
            return ref[c * ROWS : (c + 1) * ROWS, j * LANES : (j + 1) * LANES]

        masks = [[plane(mask_ref, c, j).astype(F32) for j in range(parts)] for c in range(chunks)]
        ahead = [plane(sign_ref, chunk, j) > 0 for j in range(parts)]

        def quadrant(q):
            east = q in (1, 2)
            north = q in (2, 3)
            beside = chunk + 1 if north else chunk - 1

            def sector(d, below, above):
                def group(g, _):
                    start = pl.multiple_of(d * nfreq + g * 8, 8)
                    edges = None
                    if not 0 <= beside < chunks:
                        edges = [edge_ref[j, pl.ds(start, 8), :] for j in range(parts)]
                    for u in range(8):
                        b, f = start + u, g * 8 + u
                        here = [tiles_ref[chunk, j, b] for j in range(parts)]
                        field = [here[j] * masks[chunk][j] for j in range(parts)]
                        for j in range(parts):
                            k = j + 1 if east else j - 1
                            outer = field[k] if 0 <= k < parts else 0.0
                            if east:
                                x = pltpu.roll(jnp.where(lane == 0, outer, field[j]), LANES - 1, 1)
                            else:
                                x = pltpu.roll(jnp.where(lane == LANES - 1, outer, field[j]), 1, 1)
                            if edges is None:
                                outer = tiles_ref[beside, j, b] * masks[beside][j]
                            else:
                                outer = jnp.broadcast_to(edges[j][u : u + 1], (ROWS, LANES))
                            if north:
                                y = pltpu.roll(jnp.where(row == 0, outer, field[j]), ROWS - 1, 0)
                            else:
                                y = pltpu.roll(jnp.where(row == ROWS - 1, outer, field[j]), 1, 0)
                            upstream = jnp.where(ahead[j], below(b, f, j), above(b, f, j))
                            total = coef_ref[3 * q, b] * here[j] + coef_ref[3 * q + 1, b] * x
                            total = total + (coef_ref[3 * q + 2, b] * y + 0.3 * upstream)
                            base_ref[j, b] = total * masks[chunk][j]
                    return 0

                lax.fori_loop(0, nfreq // 8, group, 0)

            def halo(ref):
                return lambda b, f, j: ref[f, chunk * ROWS : (chunk + 1) * ROWS, j * LANES : (j + 1) * LANES]

            def inside(shift):
                return lambda b, f, j: tiles_ref[chunk, j, b + shift]

            sector(0, halo(low_ref), inside(nfreq))

            def middle(d, _):
                sector(d, inside(-nfreq), inside(nfreq))
                return 0

            lax.fori_loop(1, ndir - 1, middle, 0)
            sector(ndir - 1, inside(-nfreq), halo(high_ref))

        for q in range(4):
            pl.when(place == q)(lambda q=q: quadrant(q))
        for copy in copies:
            copy.wait()

    cells = parts * ROWS * LANES
    return call(
        body,
        [(place, SMEM), (coef, SMEM)]
        + [(v, VMEM) for v in (tiles, low, high, edge, mask, sign)]
        + [(count, SMEM), (target, HBM)],
        [
            ((parts, bins, ROWS, LANES), F32),
            ((parts, bins, ROWS, LANES), F32),
            ((1, cells // 2), F32),
            ((1, cells // 2), F32),
            ((1, cells // 2), F32),
        ],
        (40 * bins * cells, 8 * bins * cells),
        scratch=[pltpu.SemaphoreType.DMA((parts,))],
        after=after,
        limit=32,
        name="stencil",
    )


def decode(place, hid, w_out, base, goal, mask, count, seed, chunk, own, after=()):
    parts, bins = base.shape[:2]
    hidden = w_out.shape[1]
    half = ROWS // 2
    wide = half * LANES
    cells = parts * wide
    seeds = [seed] if seed is not None else []

    def body(place_ref, count_ref, hid_ref, w_ref, base_ref, goal_ref, mask_ref, *refs):
        next_ref, grad_ref, out_ref, unit_ref, back_ref = refs[len(seeds) :]
        core = place_ref[0] % 2
        first = first_row(core, own)
        unit_ref[...] = jnp.full(unit_ref.shape, 1.0 / PRE_SCALE, F32)
        total = refs[0][...] if seeds else jnp.zeros(grad_ref.shape, F32)
        for j in range(parts):
            base = base_ref.at[j].reshape(bins * ROWS, LANES)
            goal = goal_ref.at[j].reshape(bins * ROWS, LANES)
            result = next_ref.at[j].reshape(bins * ROWS, LANES)
            hid = hid_ref[:, j * wide : (j + 1) * wide]
            source = jnp.dot(w_ref[...], hid, preferred_element_type=F32)
            for i in range(half):
                at = pl.ds(first + i, bins, stride=ROWS)
                mask = pick(mask_ref, core, own, chunk, i, j)
                weight = (1.0 / count_of(count_ref, core, own, chunk, i)) * mask
                part = source[:, i * LANES : (i + 1) * LANES]
                new = base[at, :] + (0.5 * mask) * part
                result[at, :] = new
                back_ref[:, i * LANES : (i + 1) * LANES] = (weight * (new - goal[at, :])).astype(BF16)
            back = back_ref[...]
            total = total + lax.dot_general(back, hid, (((1,), (1,)), ((), ())), preferred_element_type=F32)
            out_ref[:, j * wide : (j + 1) * wide] = lax.dot_general(
                w_ref[...], back, (((0,), (0,)), ((), ())), preferred_element_type=F32
            )
        grad_ref[...] = total

    return call(
        body,
        [(place, SMEM), (count, SMEM)] + [(v, VMEM) for v in (hid, w_out, base, goal, mask, *seeds)],
        [(base.shape, F32), ((bins, hidden), F32), ((hidden, cells), F32), ((1, cells), F32)],
        (6 * bins * hidden * cells, 12 * bins * cells),
        scratch=[pltpu.VMEM((bins, wide), BF16)],
        aliases={4: 0},
        after=after,
        name="decode",
    )


def store(nexts, rows, after=()):
    parts, bins = nexts[0].shape[:2]
    n = len(nexts)

    def body(*refs):
        copies = []
        for c in range(n):
            for j in range(parts):
                to = refs[n].at[:, pl.ds(c * ROWS, ROWS), pl.ds(j * LANES, LANES)]
                copies.append(pltpu.make_async_copy(refs[c].at[j], to, refs[n + 1].at[c * parts + j]))
        for copy in copies:
            copy.start()
        for copy in copies:
            copy.wait()

    size = bins * rows * parts * LANES
    return call(
        body,
        [(v, VMEM) for v in nexts],
        [((bins, rows, parts * LANES), F32, HBM)],
        (0, 8 * size),
        scratch=[pltpu.SemaphoreType.DMA((n * parts,))],
        after=after,
        name="store",
    )[0]


def write_packed(ref, total):
    n = total.shape[0]
    most = jnp.max(jnp.max(jnp.abs(total), axis=1, keepdims=True), axis=0, keepdims=True)
    power = jnp.ceil(jnp.log2(jnp.maximum(most, 2.0**-100)))
    ref[0:n, :] = total
    ref[n:, :] = jnp.broadcast_to(power, (POWER_ROWS, total.shape[1]))


def pack(total, after=()):
    def body(total_ref, out_ref):
        write_packed(out_ref, total_ref[...])

    n, width = total.shape
    return call(
        body, [(total, VMEM)], [((n + POWER_ROWS, width), F32)], (n * width, 8 * n * width), after=after, name="pack"
    )[0]


def collect(spec, back, seed, last=False, after=()):
    bins, cells = spec.shape
    hidden = back.shape[0]
    seeds = [seed] if seed is not None else []

    def body(spec_ref, back_ref, *refs):
        total = lax.dot_general(spec_ref[...], back_ref[...], (((1,), (1,)), ((), ())), preferred_element_type=F32)
        if seeds:
            total = total + refs[0][...]
        if last:
            write_packed(refs[-1], total)
        else:
            refs[-1][...] = total

    return call(
        body,
        [(v, VMEM) for v in (spec, back, *seeds)],
        [((bins + (POWER_ROWS if last else 0), hidden), F32)],
        (2 * bins * hidden * cells, 2 * bins * cells + 2 * hidden * cells),
        after=after,
        name="collect",
    )[0]


def space_sum(packed):
    n = packed.shape[0] - POWER_ROWS
    body = lax.broadcasted_iota(jnp.int32, packed.shape, 0) < n
    count = lax.axis_size("space")
    assert count & (count - 1) == 0
    total = packed
    bit = 1
    while bit < count:
        power = total[n : n + 1]
        mine = jnp.where(body, total * jnp.exp2(-power), total).astype(F16)
        other = swap(mine, "space", bit)
        mine, other = mine.astype(F32), other.astype(F32)
        here, there = mine[n : n + 1], other[n : n + 1]
        total = jnp.where(
            body, mine * jnp.exp2(here) + other * jnp.exp2(there), jnp.maximum(mine, other) + 1.0
        )
        bit *= 2
    return total[:n]


def courant(sectors, ndir, nfreq):
    angle = 2.0 * math.pi * (np.arange(NDIR) + 0.5) / NDIR
    speed = 1.0 / (1.0 + 2.3 * np.arange(nfreq) / nfreq)
    cx = np.abs(0.4 * np.cos(angle)[:, None] * speed[None, :])
    cy = np.abs(0.4 * np.sin(angle)[:, None] * speed[None, :])
    table = np.stack([1.0 - cx - cy - 0.3, cx, cy]).reshape(3, sectors, ndir * nfreq)
    return np.ascontiguousarray(table.transpose(1, 0, 2).reshape(3 * sectors, ndir * nfreq), np.float32)


def on_device(state, target, w_in, w_out, sea_mask, sea_count, turn_sign):
    ndir, nfreq, rows, lon = state.shape
    bins = ndir * nfreq
    hidden = w_in.shape[2]
    place = lax.axis_index("dir")
    sectors = lax.axis_size("dir")
    spaces = lax.axis_size("space")
    assert sectors == 4 and ndir * sectors == NDIR
    chunks, parts = rows // ROWS, lon // LANES
    upper = place % 2 == 1
    north = place >= sectors // 2
    place_ref = place.reshape(1)
    state = state.reshape(bins, rows, lon)
    target = target.reshape(bins, rows, lon)
    w_in = w_in.reshape(bins, hidden)
    w_out = jnp.transpose(w_out, (1, 2, 0)).reshape(bins, hidden)
    coef = jnp.asarray(courant(sectors, ndir, nfreq))

    def edge_bin(first):
        start = jnp.where(first, 0, bins - nfreq)
        return lax.dynamic_slice_in_dim(state, start, nfreq, 0).astype(F16)

    far = swap(edge_bin(jnp.logical_not(upper)), "dir", 3)
    near = swap(edge_bin(upper), "dir", 1)
    at = jnp.where(north, 0, rows - 1)
    edge = lax.dynamic_index_in_dim(state, at, 1, False)
    edge = edge * lax.dynamic_index_in_dim(sea_mask, at, 0, True).astype(F32)
    pairs = []
    for s in range(spaces):
        for d in range(sectors):
            to = s - 1 if d >= sectors // 2 else s + 1
            if 0 <= to < spaces:
                pairs.append((s * sectors + d, to * sectors + d))
    edge = lax.ppermute(edge.astype(F16), ("space", "dir"), pairs).astype(F32)
    edge = jnp.stack([edge[:, j * LANES : (j + 1) * LANES] for j in range(parts)])
    low = jnp.where(upper, near, far).astype(F32)
    high = jnp.where(upper, far, near).astype(F32)

    tiles, spec, send = encode_first(place_ref, state, sea_mask, w_in)
    specs, owns, sends = {(0, 0): spec}, [], [send]
    for c in range(chunks):
        for own in (0, 1):
            if (c, own) not in specs:
                specs[c, own], out = encode(place_ref, tiles, sea_mask, w_in, c, bool(own))
                (owns if own else sends).append(out)
    chips = [((owns[c] + swap(sends[c], "dir", 1)) * PRE_SCALE).astype(F16) for c in range(chunks)]

    stencils = []
    for c in range(chunks):
        stencils.append(
            stencil(
                place_ref, coef, tiles, low, high, edge, sea_mask, turn_sign, sea_count, target, c, ndir,
                after=owns[-1:] if c == 0 else [stencils[-1][2]],
            )
        )
    unit = stencils[-1][2]

    grad_out = None
    backs, slopes, nexts, tokens = [], [], [], []
    for c in range(chunks):
        base, goal, _, down, up = stencils[c]
        pre = (chips[c].astype(F32) + swap(chips[c], "dir", 2).astype(F32)) * unit
        hid = jax.nn.silu(pre).astype(BF16)
        sig = jax.nn.sigmoid(pre)
        slopes.append(swap(sig * (1.0 + pre * (1.0 - sig)), "dir", 1))
        other = swap(hid, "dir", 1)
        base, grad_out, send, _ = decode(
            place_ref, hid, w_out, base, goal, sea_mask, sea_count, grad_out, c, True, after=tokens[-1:]
        )
        base, grad_out, own, unit = decode(
            place_ref, other, w_out, base, goal, sea_mask, sea_count, grad_out, c, False
        )
        nexts.append(base)
        backs.append((((own + swap(send, "dir", 1)) * down).astype(F16), up))
        tokens.append(backs[-1][0][:8, :LANES].astype(F32))

    next_state = store(nexts, rows, after=tokens[-1:])
    grad_out = space_sum(pack(grad_out, after=tokens[-1:]))

    grad_in = None
    for c in range(chunks):
        chip, up = backs[c]
        back = (chip.astype(F32) + swap(chip, "dir", 2).astype(F32)) * up
        back = (back * slopes[c]).astype(BF16)
        last = c + 1 == chunks
        grad_in = collect(specs[c, 0], back, grad_in, after=[grad_out] if last else [])
        grad_in = collect(specs[c, 1], swap(back, "dir", 1), grad_in, last=last)

    grad_in = space_sum(grad_in)
    return (
        next_state.reshape(ndir, nfreq, rows, lon),
        grad_in.reshape(ndir, nfreq, hidden),
        jnp.transpose(grad_out.reshape(ndir, nfreq, hidden), (2, 0, 1)),
    )


def solution(mesh):
    in_specs = (
        P("dir", None, "space", None),
        P("dir", None, "space", None),
        P("dir", None, None),
        P(None, "dir", None),
        P("space", None),
        P("space"),
        P("space", None),
    )
    out_specs = (P("dir", None, "space", None), P("dir", None, None), P(None, "dir", None))
    return jax.shard_map(
        on_device, mesh=mesh, in_specs=in_specs, out_specs=out_specs, check_vma=False
    )
```

```python
import math

import jax
import jax.numpy as jnp
import numpy as np
from jax import lax
from jax.experimental import pallas as pl
from jax.experimental.pallas import tpu as pltpu
from jax.sharding import PartitionSpec as P

NDIR = 36
ROWS = 8
LANES = 128
PRE_SCALE = 64.0
BACK_SCALE = 2.0**-8
LIMIT1 = 16
POWER_ROWS = 16

BF16, F16, F32 = jnp.bfloat16, jnp.float16, jnp.float32
VMEM = pl.BlockSpec(memory_space=pltpu.VMEM)
SMEM = pl.BlockSpec(memory_space=pltpu.SMEM)
HBM = pl.BlockSpec(memory_space=pltpu.HBM)
ANY = pl.BlockSpec(memory_space=pl.ANY)
FREE = pl.BlockSpec(memory_space=pltpu.VMEM)


def swap(value, axis, bit):
    count = lax.axis_size(axis)
    return lax.ppermute(value, axis, [(i, i ^ bit) for i in range(count)])


def call(body, ins, outs, cost, after=(), aliases=None, scratch=(), limit=16, name=None):
    n = len(ins)

    def run(*refs):
        body(*refs[:n], *refs[n + len(after) :])

    def placed(dims, dtype, spec=VMEM):
        if spec is FREE:
            return jax.ShapeDtypeStruct(dims, dtype)
        return (pltpu.HBM if spec is HBM else pltpu.VMEM)(dims, dtype)

    values = [pltpu.with_memory_space_constraint(v, pltpu.HBM) if spec is HBM else v for v, spec in ins]
    return pl.pallas_call(
        run,
        in_specs=[spec for _, spec in ins] + [ANY] * len(after),
        out_specs=[VMEM if len(out) == 2 else out[2] for out in outs],
        out_shape=[placed(*out) for out in outs],
        scratch_shapes=list(scratch),
        input_output_aliases=aliases or {},
        compiler_params=pltpu.CompilerParams(vmem_limit_bytes=limit << 20),
        name=name,
    )(*values, *after)


def first_row(core, own):
    half = ROWS // 2
    return core * half if own else (1 - core) * half


def pick(ref, core, own, chunk, i, j):
    at = chunk * ROWS + i
    lanes = slice(j * LANES, (j + 1) * LANES)
    low, high = ref[at : at + 1, lanes], ref[at + ROWS // 2 : at + ROWS // 2 + 1, lanes]
    return jnp.where((core == 0) == own, low, high).astype(F32)


def count_of(count_ref, core, own, chunk, i):
    value = count_ref[chunk * ROWS + first_row(core, own) + i]
    return jnp.full((1, LANES), value, jnp.int32).astype(F32)


def write_columns(refs, start, value):
    offset = 0
    for ref in refs:
        for k in range(value.shape[1] // LANES):
            at = start + k * LANES - offset
            if 0 <= at < ref.shape[1]:
                ref[:, at : at + LANES] = value[:, k * LANES : (k + 1) * LANES]
        offset += ref.shape[1]


def read_columns(refs, start, width):
    found, offset = [], 0
    for ref in refs:
        low, high = max(start - offset, 0), min(start + width - offset, ref.shape[1])
        if low < high:
            found.append(ref[:, low:high])
        offset += ref.shape[1]
    return found[0] if len(found) == 1 else jnp.concatenate(found, axis=1)


def pieces_of(dims, dtype, cut):
    widths = cut if isinstance(cut, tuple) else (dims[1] // cut,) * cut
    return [((dims[0], width), dtype) for width in widths]


def encode_rows(place_ref, tiles_ref, mask_ref, w_ref, spec_ref, out_refs, chunk, own):
    parts, bins = tiles_ref.shape[1:3]
    half = ROWS // 2
    wide = half * LANES
    core = place_ref[0] % 2
    first = first_row(core, own)
    for j in range(parts):
        flat = tiles_ref.at[chunk, j].reshape(bins * ROWS, LANES)
        cols = []
        for i in range(half):
            row = flat[pl.ds(first + i, bins, stride=ROWS), :]
            cols.append((row * pick(mask_ref, core, own, chunk, i, j)).astype(BF16))
        field = jnp.concatenate(cols, axis=1)
        spec_ref[:, j * wide : (j + 1) * wide] = field
        out = lax.dot_general(w_ref[...], field, (((0,), (0,)), ((), ())), preferred_element_type=F32)
        write_columns(out_refs, j * wide, out)


def encode_first(place, state, mask, w_in, cut, after=()):
    bins, rows, lon = state.shape
    hidden = w_in.shape[1]
    chunks, parts = rows // ROWS, lon // LANES
    cells = parts * ROWS * LANES // 2

    def body(place_ref, state_ref, mask_hbm, w_hbm, tiles_ref, spec_ref, *refs):
        out_refs, (mask_ref, w_ref, sems) = refs[:cut], refs[cut:]
        small = [
            pltpu.make_async_copy(a, b, sems.at[chunks * parts + k])
            for k, (a, b) in enumerate([(mask_hbm, mask_ref), (w_hbm, w_ref)])
        ]
        copies = [
            [
                pltpu.make_async_copy(
                    state_ref.at[:, pl.ds(c * ROWS, ROWS), pl.ds(j * LANES, LANES)],
                    tiles_ref.at[c, j],
                    sems.at[c * parts + j],
                )
                for j in range(parts)
            ]
            for c in range(chunks)
        ]
        for row in copies:
            for copy in row:
                copy.start()
        for copy in small:
            copy.start()
        for copy in copies[0] + small:
            copy.wait()
        encode_rows(place_ref, tiles_ref, mask_ref, w_ref, spec_ref, out_refs, 0, False)
        for row in copies[1:]:
            for copy in row:
                copy.wait()

    return call(
        body,
        [(place, SMEM), (state, HBM), (mask, HBM), (w_in, HBM)],
        [((chunks, parts, bins, ROWS, LANES), F32), ((bins, cells), BF16), *pieces_of((hidden, cells), F32, cut)]
        + [(mask.shape, mask.dtype), (w_in.shape, w_in.dtype)],
        (2 * bins * hidden * cells, 4 * bins * rows * lon),
        scratch=[pltpu.SemaphoreType.DMA((chunks * parts + 2,))],
        after=after,
        limit=LIMIT1,
        name="encode_first",
    )


def encode(place, tiles, mask, w_in, chunk, own, cut=1, after=()):
    parts, bins = tiles.shape[1:3]
    hidden = w_in.shape[1]
    cells = parts * ROWS * LANES // 2

    def body(place_ref, tiles_ref, mask_ref, w_ref, spec_ref, *out_refs):
        encode_rows(place_ref, tiles_ref, mask_ref, w_ref, spec_ref, out_refs, chunk, own)

    return call(
        body,
        [(place, SMEM), (tiles, VMEM), (mask, VMEM), (w_in, VMEM)],
        [((bins, cells), BF16)] + pieces_of((hidden, cells), F32, cut),
        (2 * bins * hidden * cells, 4 * bins * cells),
        after=after,
        name="encode",
    )


def edge_bin(place, tiles, ndir, own, after=()):
    chunks, parts, bins = tiles.shape[:3]
    nfreq = bins // ndir

    def body(place_ref, tiles_ref, out_ref):
        upper = place_ref[0] % 2
        start = pl.multiple_of((1 - upper if own else upper) * (bins - nfreq), 8)
        for c in range(chunks):
            for j in range(parts):
                out_ref[c, j] = tiles_ref[c, j, pl.ds(start, nfreq)]

    ins = [(place, SMEM), (tiles, VMEM)]
    return call(body, ins, [((chunks, parts, nfreq, ROWS, LANES), F32)], (0, 0), after=after, name="edge_bin")[0]


def edge_row(place, tiles, mask, after=()):
    chunks, parts, bins = tiles.shape[:3]

    def body(place_ref, tiles_ref, mask_ref, edge_ref):
        for north in (False, True):
            c, i = (0, 0) if north else (chunks - 1, ROWS - 1)

            @pl.when((place_ref[0] >= 2) == north)
            def _():
                for j in range(parts):
                    mask = mask_ref[c * ROWS + i : c * ROWS + i + 1, j * LANES : (j + 1) * LANES].astype(F32)
                    flat = tiles_ref.at[c, j].reshape(bins * ROWS, LANES)
                    edge_ref[j] = flat[pl.ds(i, bins, stride=ROWS), :] * mask

    ins = [(place, SMEM), (tiles, VMEM), (mask, VMEM)]
    return call(body, ins, [((parts, bins, LANES), F32)], (0, 0), after=after, name="edge_row")[0]


def join(own, received, scale, cut, after=()):
    n, m = len(own), len(received)
    rows, width = own[0].shape[0], n * own[0].shape[1]

    def body(scale_ref, *refs):
        for k in range(width // LANES):
            at = slice(k * LANES, (k + 1) * LANES)
            total = read_columns(refs[:n], k * LANES, LANES) + read_columns(refs[n : n + m], k * LANES, LANES)
            write_columns(refs[n + m :], k * LANES, total * scale_ref[:, at])

    values = [(v, VMEM) for v in (scale, *own, *received)]
    return call(body, values, pieces_of((rows, width), F32, cut), (0, 0), after=after, name="join")


def cross(pieces):
    return [swap(v.astype(F16), "dir", 2).astype(F32) for v in pieces]


def activate(own, received, cut, after=()):
    n = len(own)
    rows, width = own[0].shape[0], n * own[0].shape[1]

    def body(*refs):
        own_refs, received_refs, slope_ref, hid_refs = refs[:n], refs[n : 2 * n], refs[2 * n], refs[2 * n + 1 :]
        for k in range(width // LANES):
            at = slice(k * LANES, (k + 1) * LANES)
            pre = read_columns(own_refs, k * LANES, LANES) + read_columns(received_refs, k * LANES, LANES)
            pre = pre * (1.0 / PRE_SCALE)
            sig = 1.0 / (1.0 + jnp.exp(-pre))
            slope_ref[:, at] = sig * (1.0 + pre * (1.0 - sig))
            write_columns(hid_refs, k * LANES, (pre * sig).astype(BF16))

    outs = [((rows, width), F32), *pieces_of((rows, width), BF16, cut)]
    slope, *hid = call(body, [(v, VMEM) for v in (*own, *received)], outs, (0, 0), after=after, name="activate")
    return hid, slope


def slope_back(own, received, up, slope, cut, after=()):
    n = len(own)

    def body(up_ref, slope_ref, *refs):
        for k in range(slope.shape[1] // LANES):
            at = slice(k * LANES, (k + 1) * LANES)
            total = read_columns(refs[:n], k * LANES, LANES) + read_columns(refs[n : 2 * n], k * LANES, LANES)
            write_columns(refs[2 * n :], k * LANES, (total * up_ref[:, at] * slope_ref[:, at]).astype(BF16))

    values = [(v, VMEM) for v in (up, slope, *own, *received)]
    return call(body, values, pieces_of(slope.shape, BF16, cut), (0, 0), after=after, name="slope_back")


def stencil(place, coef, tiles, near, mask, sign, count, target, extra, chunk, ndir, after=()):
    chunks, parts, bins = tiles.shape[:3]
    nfreq = bins // ndir
    half = ROWS // 2
    wide = half * LANES

    def body(
        place_ref, coef_ref, tiles_ref, near_ref, mask_ref, sign_ref, count_ref, target_ref, extra_ref,
        base_ref, goal_ref, down_ref, up_ref, kept_ref, sems,
    ):
        copies = []
        for j in range(parts):
            copy = pltpu.make_async_copy(
                target_ref.at[:, pl.ds(chunk * ROWS, ROWS), pl.ds(j * LANES, LANES)], goal_ref.at[j], sems.at[j]
            )
            copy.start()
            copies.append(copy)
        copies.append(pltpu.make_async_copy(extra_ref, kept_ref, sems.at[parts]))
        copies[-1].start()
        place = place_ref[0]
        for i in range(half):
            counts = count_of(count_ref, place % 2, True, chunk, i)
            for j in range(parts):
                at = slice(j * wide + i * LANES, j * wide + (i + 1) * LANES)
                down_ref[:, at] = counts * BACK_SCALE
                up_ref[:, at] = (1.0 / BACK_SCALE) / counts
        lane = lax.broadcasted_iota(jnp.int32, (ROWS, LANES), 1)
        row = lax.broadcasted_iota(jnp.int32, (ROWS, LANES), 0)

        def plane(ref, c, j):
            return ref[c * ROWS : (c + 1) * ROWS, j * LANES : (j + 1) * LANES]

        masks = [[plane(mask_ref, c, j).astype(F32) for j in range(parts)] for c in range(chunks)]
        ahead = [plane(sign_ref, chunk, j) > 0 for j in range(parts)]

        def quadrant(q):
            east = q in (1, 2)
            north = q in (2, 3)
            beside = chunk + 1 if north else chunk - 1

            def sector(d, below, above):
                def group(g, _):
                    start = pl.multiple_of(d * nfreq + g * 8, 8)
                    for u in range(8):
                        b, f = start + u, g * 8 + u
                        here = [tiles_ref[chunk, j, b] for j in range(parts)]
                        field = [here[j] * masks[chunk][j] for j in range(parts)]
                        for j in range(parts):
                            k = j + 1 if east else j - 1
                            outer = field[k] if 0 <= k < parts else 0.0
                            if east:
                                x = pltpu.roll(jnp.where(lane == 0, outer, field[j]), LANES - 1, 1)
                            else:
                                x = pltpu.roll(jnp.where(lane == LANES - 1, outer, field[j]), 1, 1)
                            outer = 0.0
                            if 0 <= beside < chunks:
                                outer = tiles_ref[beside, j, b] * masks[beside][j]
                            if north:
                                y = pltpu.roll(jnp.where(row == 0, outer, field[j]), ROWS - 1, 0)
                            else:
                                y = pltpu.roll(jnp.where(row == ROWS - 1, outer, field[j]), 1, 0)
                            upstream = jnp.where(ahead[j], below(b, f, j), above(b, f, j))
                            total = coef_ref[3 * q, b] * here[j] + coef_ref[3 * q + 1, b] * x
                            total = total + (coef_ref[3 * q + 2, b] * y + 0.3 * upstream)
                            base_ref[j, b] = total * masks[chunk][j]
                    return 0

                lax.fori_loop(0, nfreq // 8, group, 0)

            def far(b, f, j):
                return jnp.zeros((ROWS, LANES), F32)

            def near(b, f, j):
                return near_ref[chunk, j, f]

            def inside(shift):
                return lambda b, f, j: tiles_ref[chunk, j, b + shift]

            sector(0, near if q % 2 else far, inside(nfreq))

            def middle(d, _):
                sector(d, inside(-nfreq), inside(nfreq))
                return 0

            lax.fori_loop(1, ndir - 1, middle, 0)
            sector(ndir - 1, inside(-nfreq), far if q % 2 else near)

        for q in range(4):
            pl.when(place == q)(lambda q=q: quadrant(q))
        for copy in copies:
            copy.wait()

    cells = parts * ROWS * LANES
    return call(
        body,
        [(place, SMEM), (coef, SMEM)]
        + [(v, VMEM) for v in (tiles, near, mask, sign)]
        + [(count, SMEM), (target, HBM), (extra, HBM)],
        [
            ((parts, bins, ROWS, LANES), F32),
            ((parts, bins, ROWS, LANES), F32),
            ((1, cells // 2), F32),
            ((1, cells // 2), F32),
            (extra.shape, extra.dtype),
        ],
        (40 * bins * cells, 8 * bins * cells),
        scratch=[pltpu.SemaphoreType.DMA((parts + 1,))],
        after=after,
        limit=32,
        name="stencil",
    )


def turn_in(place, coef, base, far, edge, mask, sign, chunk, chunks, ndir, after=()):
    parts, bins = base.shape[:2]
    nfreq = bins // ndir

    def body(place_ref, coef_ref, base_ref, far_ref, edge_ref, mask_ref, sign_ref, out_ref):
        place = place_ref[0]
        upper = place % 2
        start = pl.multiple_of(upper * (bins - nfreq), 8)
        for j in range(parts):
            at = (slice(chunk * ROWS, (chunk + 1) * ROWS), slice(j * LANES, (j + 1) * LANES))
            ahead = jnp.where(sign_ref[at] > 0, 1, 0)
            share = jnp.where(ahead != upper, 0.3 * mask_ref[at].astype(F32), 0.0)
            bin_edge = pl.ds(start, nfreq)
            out_ref[j, bin_edge] = base_ref[j, bin_edge] + share[None] * far_ref[chunk, j]
        freq = lax.broadcasted_iota(jnp.int32, (nfreq, LANES), 0).astype(F32)
        speed = 1.0 / (1.0 + 2.3 * freq / nfreq)

        def blow(i):
            for j in range(parts):
                flat = out_ref.at[j].reshape(bins * ROWS, LANES)
                lanes = slice(j * LANES, (j + 1) * LANES)
                mask = mask_ref[chunk * ROWS + i : chunk * ROWS + i + 1, lanes].astype(F32)
                for d in range(ndir):
                    at = pl.ds(d * nfreq * ROWS + i, nfreq, stride=ROWS)
                    cy = coef_ref[3 * place + 2, d * nfreq] * speed
                    flat[at, :] = flat[at, :] + (mask * cy) * edge_ref[j, d * nfreq : (d + 1) * nfreq, :]

        if chunk == 0:
            pl.when(place < 2)(lambda: blow(0))
        if chunk == chunks - 1:
            pl.when(place >= 2)(lambda: blow(ROWS - 1))

    ins = [(place, SMEM), (coef, SMEM)] + [(v, VMEM) for v in (base, far, edge, mask, sign)]
    return call(body, ins, [(base.shape, F32)], (0, 0), after=after, aliases={2: 0}, name="turn_in")[0]


def decode(place, hid, w_out, base, goal, mask, count, seed, chunk, own, which, cut=1, after=()):
    bins = base.shape[1]
    hidden = w_out.shape[1]
    half = ROWS // 2
    wide = half * LANES
    cells = len(which) * wide
    seeds = [seed] if seed is not None else []

    def body(place_ref, count_ref, w_ref, base_ref, goal_ref, mask_ref, *refs):
        hid_refs, refs = refs[: len(hid)], refs[len(hid) :]
        next_ref, grad_ref, *out_refs, back_ref = refs[len(seeds) :]
        core = place_ref[0] % 2
        first = first_row(core, own)
        total = refs[0][...] if seeds else jnp.zeros(grad_ref.shape, F32)
        for k, j in enumerate(which):
            base = base_ref.at[j].reshape(bins * ROWS, LANES)
            goal = goal_ref.at[j].reshape(bins * ROWS, LANES)
            result = next_ref.at[j].reshape(bins * ROWS, LANES)
            units = read_columns(hid_refs, j * wide, wide)
            source = jnp.dot(w_ref[...], units, preferred_element_type=F32)
            for i in range(half):
                at = pl.ds(first + i, bins, stride=ROWS)
                mask = pick(mask_ref, core, own, chunk, i, j)
                weight = (1.0 / count_of(count_ref, core, own, chunk, i)) * mask
                part = source[:, i * LANES : (i + 1) * LANES]
                new = base[at, :] + (0.5 * mask) * part
                result[at, :] = new
                back_ref[:, i * LANES : (i + 1) * LANES] = (weight * (new - goal[at, :])).astype(BF16)
            back = back_ref[...]
            total = total + lax.dot_general(back, units, (((1,), (1,)), ((), ())), preferred_element_type=F32)
            out = lax.dot_general(w_ref[...], back, (((0,), (0,)), ((), ())), preferred_element_type=F32)
            write_columns(out_refs, k * wide, out)
        grad_ref[...] = total

    return call(
        body,
        [(place, SMEM), (count, SMEM)] + [(v, VMEM) for v in (w_out, base, goal, mask, *hid, *seeds)],
        [(base.shape, F32), ((bins, hidden), F32)]
        + pieces_of((hidden, cells), F32, cut),
        (6 * bins * hidden * cells, 12 * bins * cells),
        scratch=[pltpu.VMEM((bins, wide), BF16)],
        aliases={3: 0},
        after=after,
        name="decode",
    )


def store(nexts, rows, after=()):
    parts, bins = nexts[0].shape[:2]
    n = len(nexts)

    def body(*refs):
        copies = []
        for c in range(n):
            for j in range(parts):
                to = refs[n].at[:, pl.ds(c * ROWS, ROWS), pl.ds(j * LANES, LANES)]
                copies.append(pltpu.make_async_copy(refs[c].at[j], to, refs[n + 2].at[c * parts + j]))
        for copy in copies:
            copy.start()
        refs[n + 1][...] = jnp.zeros(refs[n + 1].shape, F32)
        for copy in copies:
            copy.wait()

    size = bins * rows * parts * LANES
    return call(
        body,
        [(v, VMEM) for v in nexts],
        [((bins, rows, parts * LANES), F32, HBM), ((ROWS, LANES), F32)],
        (0, 8 * size),
        scratch=[pltpu.SemaphoreType.DMA((n * parts,))],
        after=after,
        name="store",
    )


def write_packed(ref, total):
    n = total.shape[0]
    most = jnp.max(jnp.max(jnp.abs(total), axis=1, keepdims=True), axis=0, keepdims=True)
    power = jnp.ceil(jnp.log2(jnp.maximum(most, 2.0**-100)))
    ref[0:n, :] = total
    ref[n:, :] = jnp.broadcast_to(power, (POWER_ROWS, total.shape[1]))


def write_scaled(refs, total, power):
    n, width = total.shape
    value = jnp.concatenate([total * jnp.exp2(-power), jnp.broadcast_to(power, (POWER_ROWS, width))], axis=0)
    write_columns(refs, 0, value)


def write_packed(refs, total):
    most = jnp.max(jnp.max(jnp.abs(total), axis=1, keepdims=True), axis=0, keepdims=True)
    power = jnp.ceil(jnp.log2(jnp.maximum(most, 2.0**-100)))
    write_scaled(refs, total, jnp.broadcast_to(power, (1, total.shape[1])))


def pack(total, cut, after=()):
    def body(total_ref, *out_refs):
        write_packed(out_refs, total_ref[...])

    n, width = total.shape
    outs = pieces_of((n + POWER_ROWS, width), F32, cut)
    return call(body, [(total, VMEM)], outs, (0, 0), after=after, name="pack")


def collect(spec, back, seed, cut=0, after=()):
    bins, cells = spec.shape
    hidden = back[0].shape[0]
    seeds = [seed] if seed is not None else []

    def body(spec_ref, *refs):
        values = read_columns(refs[: len(back)], 0, cells)
        total = lax.dot_general(spec_ref[...], values, (((1,), (1,)), ((), ())), preferred_element_type=F32)
        if seeds:
            total = total + refs[len(back)][...]
        if cut:
            write_packed(refs[len(back) + len(seeds) :], total)
        else:
            refs[-1][...] = total

    return call(
        body,
        [(v, VMEM) for v in (spec, *back, *seeds)],
        pieces_of((bins + POWER_ROWS, hidden), F32, cut) if cut else [((bins, hidden), F32)],
        (2 * bins * hidden * cells, 2 * bins * cells + 2 * hidden * cells),
        after=after,
        name="collect",
    )


def merge(mine, other, spare, after=()):
    rows, width = mine.shape
    n = rows - POWER_ROWS

    def body(mine_ref, other_ref, out_ref):
        here, there = mine_ref[n : n + 1], other_ref[n : n + 1]
        total = mine_ref[0:n] * jnp.exp2(here) + other_ref[0:n] * jnp.exp2(there)
        write_scaled([out_ref.at[0:rows]], total, jnp.maximum(here, there) + 1.0)
        if spare:
            out_ref[rows:] = jnp.zeros((spare, width), F32)

    values = [(mine, VMEM), (other, VMEM)]
    return call(body, values, [((rows + spare, width), F32)], (0, 0), after=after, name="merge")[0]


def merge_last(mine, other, n, after=()):
    k = len(mine)
    width = sum(v.shape[1] for v in mine)

    def body(*refs):
        out_ref, done_ref = refs[2 * k :]
        at = 0
        for a, b in zip(refs[:k], refs[k : 2 * k]):
            here, there = a[n : n + 1], b[n : n + 1]
            out_ref[:, at : at + a.shape[1]] = a[0:n] * jnp.exp2(here) + b[0:n] * jnp.exp2(there)
            at += a.shape[1]
        done_ref[...] = jnp.zeros(done_ref.shape, F32)

    values = [(v, VMEM) for v in (*mine, *other)]
    outs = [((n, width), F32, FREE), ((ROWS, LANES), F32)]
    return call(body, values, outs, (0, 0), after=after, name="merge_last")


def space_sum(packed, spare=0):
    n = packed[0].shape[0] - POWER_ROWS
    count = lax.axis_size("space")
    assert count & (count - 1) == 0 and count > 1
    bit = 1
    while True:
        mine = [lax.optimization_barrier(v.astype(F16)) for v in packed]
        other = [swap(v, "space", bit).astype(F32) for v in mine]
        mine = [v.astype(F32) for v in mine]
        bit *= 2
        after = yield packed[0]
        if bit >= count:
            yield merge_last(mine, other, n, after)
            return
        packed = [merge(a, b, spare if 2 * bit >= count else 0, after) for a, b in zip(mine, other)]


def courant(sectors, ndir, nfreq):
    angle = 2.0 * math.pi * (np.arange(NDIR) + 0.5) / NDIR
    speed = 1.0 / (1.0 + 2.3 * np.arange(nfreq) / nfreq)
    cx = np.abs(0.4 * np.cos(angle)[:, None] * speed[None, :])
    cy = np.abs(0.4 * np.sin(angle)[:, None] * speed[None, :])
    table = np.stack([1.0 - cx - cy - 0.3, cx, cy]).reshape(3, sectors, ndir * nfreq)
    return np.ascontiguousarray(table.transpose(1, 0, 2).reshape(3 * sectors, ndir * nfreq), np.float32)


def on_device(state, target, w_in, w_out, sea_mask, sea_count, turn_sign):
    ndir, nfreq, rows, lon = state.shape
    bins = ndir * nfreq
    hidden = w_in.shape[2]
    place = lax.axis_index("dir")
    sectors = lax.axis_size("dir")
    spaces = lax.axis_size("space")
    assert sectors == 4 and ndir * sectors == NDIR
    chunks, parts = rows // ROWS, lon // LANES
    place_ref = place.reshape(1)
    state = state.reshape(bins, rows, lon)
    target = target.reshape(bins, rows, lon)
    w_in = w_in.reshape(bins, hidden)
    w_out = jnp.transpose(w_out, (1, 2, 0)).reshape(bins, hidden)
    coef = jnp.asarray(courant(sectors, ndir, nfreq))

    tiles, spec, *send, mask, w_in = encode_first(place_ref, state, sea_mask, w_in, 4)
    pairs = []
    for s in range(spaces):
        for d in range(sectors):
            to = s - 1 if d >= sectors // 2 else s + 1
            if 0 <= to < spaces:
                pairs.append((s * sectors + d, to * sectors + d))
    near = swap(edge_bin(place_ref, tiles, ndir, True).astype(F16), "dir", 1).astype(F32)

    first = jnp.full((1, spec.shape[1]), PRE_SCALE, F32)
    specs, chips, crossed = [spec], [], []
    after = []
    for c in range(chunks):
        if c > 0:
            spec, *send = encode(place_ref, tiles, mask, w_in, c, False, 4, after=after)
            specs.append(spec)
            after = [spec]
        received = [swap(v, "dir", 1) for v in send]
        spec, own = encode(place_ref, tiles, mask, w_in, c, True, after=after)
        specs.append(spec)
        chips.append(join([own], received, first, 1))
        crossed.append(cross(chips[c]))
        after = chips[c][:1]

    far = edge_bin(place_ref, tiles, ndir, False, after=chips[0])
    far = swap(far.astype(F16), "dir", 3).astype(F32)
    edge = edge_row(place_ref, tiles, mask, after=chips[0])
    edge = lax.ppermute(edge.astype(F16), ("space", "dir"), pairs).astype(F32)

    stencils = []
    for c in range(chunks):
        stencils.append(
            stencil(
                place_ref, coef, tiles, near, mask, turn_sign, sea_count, target, [w_out, turn_sign][c % 2], c, ndir,
                after=[stencils[-1][0]] if c else chips[0],
            )
        )
    w_out = stencils[0][-1]
    after = [stencils[-1][0]]

    grad_out = None
    slopes, nexts, backs, back_crossed = [], [], [], []
    for c in range(chunks):
        base, goal, down, _, _ = stencils[c]
        base = turn_in(place_ref, coef, base, far, edge, mask, turn_sign, c, chunks, ndir, after=after)
        hid, slope = activate(chips[c], crossed[c], 4, after=[base])
        slopes.append(slope)
        other = [swap(v, "dir", 1) for v in hid]
        own = []
        for mine, which in ((True, range(1)), (False, range(parts)), (True, range(1, parts))):
            base, grad_out, *out = decode(
                place_ref, hid if mine else other, w_out, base, goal, mask, sea_count, grad_out, c, mine, which,
                cut=len(which) if mine else 4,
            )
            if mine:
                own += out
            else:
                received = [swap(v, "dir", 1) for v in out]
        nexts.append(base)
        backs.append(join(own, received, down, 2 if c + 1 == chunks else 1))
        back_crossed.append(cross(backs[c]))
        after = backs[c][:1]

    out_sum = space_sum(pack(grad_out, 1), 112)
    next(out_sum)
    merged = out_sum.send(())
    next_state, stored = store(nexts, rows, after=[merged])

    grad_in = None
    after = []
    for c in range(chunks):
        last = c + 1 == chunks
        back = slope_back(
            backs[c], back_crossed[c], stencils[c][3], slopes[c], 4 if last else 2, after=after[:2]
        )
        (grad_in,) = collect(specs[2 * c + 1], back, grad_in)
        grad_in = collect(
            specs[2 * c], [swap(v, "dir", 1) for v in back], grad_in, cut=2 if last else 0
        )
        if c + 2 == chunks:
            (grad_in,) = grad_in
            waits = [stored]
            while not isinstance(merged, (tuple, list)):
                before, merged, waits = merged, out_sum.send(waits), ()
            grad_out, summed = merged
            after = [before, grad_in, summed]
        elif not last:
            (grad_in,) = grad_in

    in_sum = space_sum(grad_in)
    next(in_sum)
    merged = in_sum.send([summed])
    while not isinstance(merged, (tuple, list)):
        merged = in_sum.send(())
    grad_in = merged[0]
    return (
        next_state.reshape(ndir, nfreq, rows, lon),
        grad_in.reshape(ndir, nfreq, hidden),
        jnp.transpose(grad_out.reshape(ndir, nfreq, hidden), (2, 0, 1)),
    )


def solution(mesh):
    in_specs = (
        P("dir", None, "space", None),
        P("dir", None, "space", None),
        P("dir", None, None),
        P(None, "dir", None),
        P("space", None),
        P("space"),
        P("space", None),
    )
    out_specs = (P("dir", None, "space", None), P("dir", None, None), P(None, "dir", None))
    return jax.shard_map(
        on_device, mesh=mesh, in_specs=in_specs, out_specs=out_specs, check_vma=False
    )
```

```python
import math

import jax
import jax.numpy as jnp
import numpy as np
from jax import lax
from jax.experimental import pallas as pl
from jax.experimental.pallas import tpu as pltpu
from jax.sharding import PartitionSpec as P

NDIR = 36
ROWS = 8
LANES = 128
PRE_SCALE = 64.0
BACK_SCALE = 2.0**-8
LIMIT1 = 16
UNROLL = 32
POWER_ROWS = 16

BF16, F16, F32 = jnp.bfloat16, jnp.float16, jnp.float32
VMEM = pl.BlockSpec(memory_space=pltpu.VMEM)
SMEM = pl.BlockSpec(memory_space=pltpu.SMEM)
HBM = pl.BlockSpec(memory_space=pltpu.HBM)
ANY = pl.BlockSpec(memory_space=pl.ANY)
FREE = pl.BlockSpec(memory_space=pltpu.VMEM)


def swap(value, axis, bit):
    count = lax.axis_size(axis)
    return lax.ppermute(value, axis, [(i, i ^ bit) for i in range(count)])


def call(body, ins, outs, cost, after=(), aliases=None, scratch=(), limit=16, name=None):
    n = len(ins)

    def run(*refs):
        body(*refs[:n], *refs[n + len(after) :])

    def placed(dims, dtype, spec=VMEM):
        if spec is FREE:
            return jax.ShapeDtypeStruct(dims, dtype)
        return (pltpu.HBM if spec is HBM else pltpu.VMEM)(dims, dtype)

    values = [pltpu.with_memory_space_constraint(v, pltpu.HBM) if spec is HBM else v for v, spec in ins]
    return pl.pallas_call(
        run,
        in_specs=[spec for _, spec in ins] + [ANY] * len(after),
        out_specs=[VMEM if len(out) == 2 else out[2] for out in outs],
        out_shape=[placed(*out) for out in outs],
        scratch_shapes=list(scratch),
        input_output_aliases=aliases or {},
        compiler_params=pltpu.CompilerParams(vmem_limit_bytes=limit << 20),
        name=name,
    )(*values, *after)


def first_row(core, own):
    half = ROWS // 2
    return core * half if own else (1 - core) * half


def pick(ref, core, own, chunk, i, j):
    at = chunk * ROWS + i
    lanes = slice(j * LANES, (j + 1) * LANES)
    low, high = ref[at : at + 1, lanes], ref[at + ROWS // 2 : at + ROWS // 2 + 1, lanes]
    return jnp.where((core == 0) == own, low, high).astype(F32)


def count_of(count_ref, core, own, chunk, i):
    value = count_ref[chunk * ROWS + first_row(core, own) + i]
    return jnp.full((1, LANES), value, jnp.int32).astype(F32)


def write_columns(refs, start, value):
    offset = 0
    for ref in refs:
        for k in range(value.shape[1] // LANES):
            at = start + k * LANES - offset
            if 0 <= at < ref.shape[1]:
                ref[:, at : at + LANES] = value[:, k * LANES : (k + 1) * LANES]
        offset += ref.shape[1]


def read_columns(refs, start, width):
    found, offset = [], 0
    for ref in refs:
        low, high = max(start - offset, 0), min(start + width - offset, ref.shape[1])
        if low < high:
            found.append(ref[:, low:high])
        offset += ref.shape[1]
    return found[0] if len(found) == 1 else jnp.concatenate(found, axis=1)


def pieces_of(dims, dtype, cut):
    widths = cut if isinstance(cut, tuple) else (dims[1] // cut,) * cut
    return [((dims[0], width), dtype) for width in widths]


def encode_rows(place_ref, tiles_ref, mask_ref, w_ref, spec_ref, out_refs, chunk, own):
    parts, bins = tiles_ref.shape[:2]
    half = ROWS // 2
    wide = half * LANES
    core = place_ref[0] % 2
    first = first_row(core, own)
    for j in range(parts):
        flat = tiles_ref.at[j].reshape(bins * ROWS, LANES)
        cols = []
        for i in range(half):
            row = flat[pl.ds(first + i, bins, stride=ROWS), :]
            cols.append((row * pick(mask_ref, core, own, chunk, i, j)).astype(BF16))
        field = jnp.concatenate(cols, axis=1)
        spec_ref[:, j * wide : (j + 1) * wide] = field
        out = lax.dot_general(w_ref[...], field, (((0,), (0,)), ((), ())), preferred_element_type=F32)
        write_columns(out_refs, j * wide, out)


def block(ref, c, j, bins=slice(None)):
    return ref.at[bins, pl.ds(c * ROWS, ROWS), pl.ds(j * LANES, LANES)]


def copy_near(place, tiles_ref, near_refs, nfreq):
    start = pl.multiple_of((1 - place % 2) * (tiles_ref.shape[1] - nfreq), 8)
    for j, ref in enumerate(near_refs):
        ref[...] = tiles_ref[j, pl.ds(start, nfreq)]


def encode_first(place, state, mask, w_in, ndir, cut, after=()):
    bins, rows, lon = state.shape
    nfreq = bins // ndir
    hidden = w_in.shape[1]
    chunks, parts = rows // ROWS, lon // LANES
    cells = parts * ROWS * LANES // 2

    def body(place_ref, state_ref, mask_hbm, w_hbm, tiles_ref, far_ref, spec_ref, *refs):
        out_refs, near_refs, (mask_ref, w_ref, sems) = refs[:cut], refs[cut : cut + parts], refs[cut + parts :]
        place = place_ref[0]
        copies = [(block(state_ref, 0, j), tiles_ref.at[j]) for j in range(parts)]
        copies += [(mask_hbm, mask_ref), (w_hbm, w_ref)]
        edge = pl.ds(pl.multiple_of((place % 2) * (bins - nfreq), 8), nfreq)
        copies += [(block(state_ref, c, j, edge), far_ref.at[c, j]) for c in range(chunks) for j in range(parts)]
        copies = [pltpu.make_async_copy(*copy, sems.at[k]) for k, copy in enumerate(copies)]
        for copy in copies:
            copy.start()
        for copy in copies[: parts + 2]:
            copy.wait()
        encode_rows(place_ref, tiles_ref, mask_ref, w_ref, spec_ref, out_refs, 0, False)
        copy_near(place, tiles_ref, near_refs, nfreq)
        for copy in copies[parts + 2 :]:
            copy.wait()

    return call(
        body,
        [(place, SMEM), (state, HBM), (mask, HBM), (w_in, HBM)],
        [
            ((parts, bins, ROWS, LANES), F32),
            ((chunks, parts, nfreq, ROWS, LANES), F32),
            ((bins, cells), BF16),
            *pieces_of((hidden, cells), F32, cut),
            *[((nfreq, ROWS, LANES), F32)] * parts,
            (mask.shape, mask.dtype),
            (w_in.shape, w_in.dtype),
        ],
        (2 * bins * hidden * cells, 4 * bins * rows * lon),
        scratch=[pltpu.SemaphoreType.DMA(((1 + chunks) * parts + 2,))],
        after=after,
        name="encode_first",
    )


def load_rest(place, state, tiles, mask, ndir, after=()):
    bins, rows, lon = state.shape
    nfreq = bins // ndir
    chunks, parts = rows // ROWS, lon // LANES
    rest = chunks - 1

    def body(place_ref, state_ref, first_ref, mask_ref, *refs):
        tiles_refs, near_refs, (edge_ref, sems) = refs[:rest], refs[rest : rest + rest * parts], refs[rest + rest * parts :]
        copies = [
            pltpu.make_async_copy(block(state_ref, c + 1, j), tiles_refs[c].at[j], sems.at[c * parts + j])
            for c in range(rest)
            for j in range(parts)
        ]
        for copy in copies:
            copy.start()
        for copy in copies:
            copy.wait()
        for c in range(rest):
            copy_near(place_ref[0], tiles_refs[c], near_refs[c * parts : (c + 1) * parts], nfreq)
        for north in (False, True):
            at, i, ref = (0, 0, first_ref) if north else (rows - ROWS, ROWS - 1, tiles_refs[-1])

            @pl.when((place_ref[0] >= 2) == north)
            def _():
                for j in range(parts):
                    mask = mask_ref[at + i : at + i + 1, j * LANES : (j + 1) * LANES].astype(F32)
                    flat = ref.at[j].reshape(bins * ROWS, LANES)
                    edge_ref[j] = flat[pl.ds(i, bins, stride=ROWS), :] * mask

    outs = call(
        body,
        [(place, SMEM), (state, HBM), (tiles, VMEM), (mask, VMEM)],
        [(tiles.shape, F32)] * rest + [((nfreq, ROWS, LANES), F32)] * (rest * parts) + [((parts, bins, LANES), F32)],
        (0, 4 * bins * rows * lon),
        scratch=[pltpu.SemaphoreType.DMA((rest * parts,))],
        after=after,
        name="load_rest",
    )
    near = [outs[rest + c * parts : rest + (c + 1) * parts] for c in range(rest)]
    return outs[:rest], near, outs[-1]


def encode(place, tiles, mask, w_in, chunk, own, cut=1, after=()):
    parts, bins = tiles.shape[:2]
    hidden = w_in.shape[1]
    cells = parts * ROWS * LANES // 2

    def body(place_ref, tiles_ref, mask_ref, w_ref, spec_ref, *out_refs):
        encode_rows(place_ref, tiles_ref, mask_ref, w_ref, spec_ref, out_refs, chunk, own)

    return call(
        body,
        [(place, SMEM), (tiles, VMEM), (mask, VMEM), (w_in, VMEM)],
        [((bins, cells), BF16)] + pieces_of((hidden, cells), F32, cut),
        (2 * bins * hidden * cells, 4 * bins * cells),
        after=after,
        name="encode",
    )


def join(own, received, scale, cut, after=()):
    n, m = len(own), len(received)
    rows, width = own[0].shape[0], n * own[0].shape[1]

    def body(scale_ref, *refs):
        for k in range(width // LANES):
            at = slice(k * LANES, (k + 1) * LANES)
            total = read_columns(refs[:n], k * LANES, LANES) + read_columns(refs[n : n + m], k * LANES, LANES)
            write_columns(refs[n + m :], k * LANES, total * scale_ref[:, at])

    values = [(v, VMEM) for v in (scale, *own, *received)]
    return call(body, values, pieces_of((rows, width), F32, cut), (0, 0), after=after, name="join")


def cross(pieces):
    return [swap(v.astype(F16), "dir", 2).astype(F32) for v in pieces]


def activate(own, received, cut, after=()):
    n = len(own)
    rows, width = own[0].shape[0], n * own[0].shape[1]

    def body(*refs):
        own_refs, received_refs, slope_ref, hid_refs = refs[:n], refs[n : 2 * n], refs[2 * n], refs[2 * n + 1 :]
        for k in range(width // LANES):
            at = slice(k * LANES, (k + 1) * LANES)
            pre = read_columns(own_refs, k * LANES, LANES) + read_columns(received_refs, k * LANES, LANES)
            pre = pre * (1.0 / PRE_SCALE)
            sig = 1.0 / (1.0 + jnp.exp(-pre))
            slope_ref[:, at] = sig * (1.0 + pre * (1.0 - sig))
            write_columns(hid_refs, k * LANES, (pre * sig).astype(BF16))

    outs = [((rows, width), F32), *pieces_of((rows, width), BF16, cut)]
    slope, *hid = call(body, [(v, VMEM) for v in (*own, *received)], outs, (0, 0), after=after, name="activate")
    return hid, slope


def slope_back(own, received, up, slope, cut, after=()):
    n = len(own)

    def body(up_ref, slope_ref, *refs):
        for k in range(slope.shape[1] // LANES):
            at = slice(k * LANES, (k + 1) * LANES)
            total = read_columns(refs[:n], k * LANES, LANES) + read_columns(refs[n : 2 * n], k * LANES, LANES)
            write_columns(refs[2 * n :], k * LANES, (total * up_ref[:, at] * slope_ref[:, at]).astype(BF16))

    values = [(v, VMEM) for v in (up, slope, *own, *received)]
    return call(body, values, pieces_of(slope.shape, BF16, cut), (0, 0), after=after, name="slope_back")


def stencil(place, coef, tiles, near, far, edge, mask, sign, count, target, extra, chunk, ndir, after=()):
    chunks = len(tiles)
    parts, bins = tiles[chunk].shape[:2]
    nfreq = bins // ndir
    half = ROWS // 2
    wide = half * LANES
    around = {c: tiles[c] for c in range(max(chunk - 1, 0), min(chunk + 2, chunks))}
    others = [far, edge] if far is not None else []

    def body(place_ref, coef_ref, count_ref, target_ref, extra_ref, mask_ref, sign_ref, *refs):
        tiles_refs = dict(zip(around, refs))
        near_refs = refs[len(around) : len(around) + parts]
        other_refs = refs[len(around) + parts : len(around) + parts + len(others)]
        base_ref, goal_ref, down_ref, up_ref, kept_ref, sems = refs[len(around) + parts + len(others) :]
        copies = []
        for j in range(parts):
            copy = pltpu.make_async_copy(
                target_ref.at[:, pl.ds(chunk * ROWS, ROWS), pl.ds(j * LANES, LANES)], goal_ref.at[j], sems.at[j]
            )
            copy.start()
            copies.append(copy)
        copies.append(pltpu.make_async_copy(extra_ref, kept_ref, sems.at[parts]))
        copies[-1].start()
        place = place_ref[0]
        for i in range(half):
            counts = count_of(count_ref, place % 2, True, chunk, i)
            for j in range(parts):
                at = slice(j * wide + i * LANES, j * wide + (i + 1) * LANES)
                down_ref[:, at] = counts * BACK_SCALE
                up_ref[:, at] = (1.0 / BACK_SCALE) / counts
        lane = lax.broadcasted_iota(jnp.int32, (ROWS, LANES), 1)
        row = lax.broadcasted_iota(jnp.int32, (ROWS, LANES), 0)

        def plane(ref, c, j):
            return ref[c * ROWS : (c + 1) * ROWS, j * LANES : (j + 1) * LANES]

        masks = [[plane(mask_ref, c, j).astype(F32) for j in range(parts)] for c in range(chunks)]
        ahead = [plane(sign_ref, chunk, j) > 0 for j in range(parts)]

        def quadrant(q):
            east = q in (1, 2)
            north = q in (2, 3)
            beside = chunk + 1 if north else chunk - 1

            def sector(d, below, above):
                def group(g, _):
                    for u in range(UNROLL):
                        b, f = d * nfreq + g * UNROLL + u, g * UNROLL + u
                        here = [tiles_refs[chunk][j, b] for j in range(parts)]
                        field = [here[j] * masks[chunk][j] for j in range(parts)]
                        for j in range(parts):
                            k = j + 1 if east else j - 1
                            outer = field[k] if 0 <= k < parts else 0.0
                            if east:
                                x = pltpu.roll(jnp.where(lane == 0, outer, field[j]), LANES - 1, 1)
                            else:
                                x = pltpu.roll(jnp.where(lane == LANES - 1, outer, field[j]), 1, 1)
                            outer = 0.0
                            if 0 <= beside < chunks:
                                outer = tiles_refs[beside][j, b] * masks[beside][j]
                            if north:
                                y = pltpu.roll(jnp.where(row == 0, outer, field[j]), ROWS - 1, 0)
                            else:
                                y = pltpu.roll(jnp.where(row == ROWS - 1, outer, field[j]), 1, 0)
                            upstream = jnp.where(ahead[j], below(b, f, j), above(b, f, j))
                            total = coef_ref[3 * q, b] * here[j] + coef_ref[3 * q + 1, b] * x
                            total = total + (coef_ref[3 * q + 2, b] * y + 0.3 * upstream)
                            base_ref[j, b] = total * masks[chunk][j]
                    return 0

                lax.fori_loop(0, nfreq // UNROLL, group, 0)

            def far_bin(b, f, j):
                return other_refs[0][chunk, j, f] if others else jnp.zeros((ROWS, LANES), F32)

            def near_bin(b, f, j):
                return near_refs[j][f]

            def inside(shift):
                return lambda b, f, j: tiles_refs[chunk][j, b + shift]

            sector(0, near_bin if q % 2 else far_bin, inside(nfreq))

            def middle(d, _):
                sector(d, inside(-nfreq), inside(nfreq))
                return 0

            lax.fori_loop(1, ndir - 1, middle, 0)
            sector(ndir - 1, inside(-nfreq), far_bin if q % 2 else near_bin)

        for q in range(4):
            pl.when(place == q)(lambda q=q: quadrant(q))
        if others:
            blow_in(place, coef_ref, other_refs[1], mask_ref, base_ref, chunk, chunks, ndir)
        for copy in copies:
            copy.wait()

    cells = parts * ROWS * LANES
    return call(
        body,
        [(place, SMEM), (coef, SMEM), (count, SMEM), (target, HBM), (extra, HBM)]
        + [(v, VMEM) for v in (mask, sign, *around.values(), *near, *others)],
        [
            ((parts, bins, ROWS, LANES), F32),
            ((parts, bins, ROWS, LANES), F32),
            ((1, cells // 2), F32),
            ((1, cells // 2), F32),
            (extra.shape, extra.dtype),
        ],
        (40 * bins * cells, 8 * bins * cells),
        scratch=[pltpu.SemaphoreType.DMA((parts + 1,))],
        after=after,
        limit=32,
        name="stencil",
    )


def blow_in(place, coef_ref, edge_ref, mask_ref, base_ref, chunk, chunks, ndir):
    parts, bins = base_ref.shape[:2]
    nfreq = bins // ndir
    freq = lax.broadcasted_iota(jnp.int32, (nfreq, LANES), 0).astype(F32)
    speed = 1.0 / (1.0 + 2.3 * freq / nfreq)

    def blow(i):
        for j in range(parts):
            flat = base_ref.at[j].reshape(bins * ROWS, LANES)
            mask = mask_ref[chunk * ROWS + i : chunk * ROWS + i + 1, j * LANES : (j + 1) * LANES].astype(F32)
            for d in range(ndir):
                at = pl.ds(d * nfreq * ROWS + i, nfreq, stride=ROWS)
                cy = coef_ref[3 * place + 2, d * nfreq] * speed
                flat[at, :] = flat[at, :] + (mask * cy) * edge_ref[j, d * nfreq : (d + 1) * nfreq, :]

    if chunk == 0:
        pl.when(place < 2)(lambda: blow(0))
    if chunk == chunks - 1:
        pl.when(place >= 2)(lambda: blow(ROWS - 1))


def turn_in(place, coef, base, far, edge, mask, sign, chunk, chunks, ndir, after=()):
    parts, bins = base.shape[:2]
    nfreq = bins // ndir

    def body(place_ref, coef_ref, base_ref, far_ref, edge_ref, mask_ref, sign_ref, out_ref):
        place = place_ref[0]
        upper = place % 2
        start = pl.multiple_of(upper * (bins - nfreq), 8)
        for j in range(parts):
            at = (slice(chunk * ROWS, (chunk + 1) * ROWS), slice(j * LANES, (j + 1) * LANES))
            ahead = jnp.where(sign_ref[at] > 0, 1, 0)
            share = jnp.where(ahead != upper, 0.3 * mask_ref[at].astype(F32), 0.0)
            bin_edge = pl.ds(start, nfreq)
            out_ref[j, bin_edge] = base_ref[j, bin_edge] + share[None] * far_ref[chunk, j]
        blow_in(place, coef_ref, edge_ref, mask_ref, out_ref, chunk, chunks, ndir)

    ins = [(place, SMEM), (coef, SMEM)] + [(v, VMEM) for v in (base, far, edge, mask, sign)]
    return call(body, ins, [(base.shape, F32)], (0, 0), after=after, aliases={2: 0}, name="turn_in")[0]


def decode(place, hid, w_out, base, goal, mask, count, seed, chunk, own, which, cut=1, after=()):
    bins = base.shape[1]
    hidden = w_out.shape[1]
    half = ROWS // 2
    wide = half * LANES
    cells = len(which) * wide
    seeds = [seed] if seed is not None else []

    def body(place_ref, count_ref, w_ref, base_ref, goal_ref, mask_ref, *refs):
        hid_refs, refs = refs[: len(hid)], refs[len(hid) :]
        next_ref, grad_ref, *out_refs, back_ref = refs[len(seeds) :]
        core = place_ref[0] % 2
        first = first_row(core, own)
        total = refs[0][...] if seeds else jnp.zeros(grad_ref.shape, F32)
        for k, j in enumerate(which):
            base = base_ref.at[j].reshape(bins * ROWS, LANES)
            goal = goal_ref.at[j].reshape(bins * ROWS, LANES)
            result = next_ref.at[j].reshape(bins * ROWS, LANES)
            units = read_columns(hid_refs, j * wide, wide)
            source = jnp.dot(w_ref[...], units, preferred_element_type=F32)
            for i in range(half):
                at = pl.ds(first + i, bins, stride=ROWS)
                mask = pick(mask_ref, core, own, chunk, i, j)
                weight = (1.0 / count_of(count_ref, core, own, chunk, i)) * mask
                part = source[:, i * LANES : (i + 1) * LANES]
                new = base[at, :] + (0.5 * mask) * part
                result[at, :] = new
                back_ref[:, i * LANES : (i + 1) * LANES] = (weight * (new - goal[at, :])).astype(BF16)
            back = back_ref[...]
            total = total + lax.dot_general(back, units, (((1,), (1,)), ((), ())), preferred_element_type=F32)
            out = lax.dot_general(w_ref[...], back, (((0,), (0,)), ((), ())), preferred_element_type=F32)
            write_columns(out_refs, k * wide, out)
        grad_ref[...] = total

    return call(
        body,
        [(place, SMEM), (count, SMEM)] + [(v, VMEM) for v in (w_out, base, goal, mask, *hid, *seeds)],
        [(base.shape, F32), ((bins, hidden), F32)]
        + pieces_of((hidden, cells), F32, cut),
        (6 * bins * hidden * cells, 12 * bins * cells),
        scratch=[pltpu.VMEM((bins, wide), BF16)],
        aliases={3: 0},
        after=after,
        name="decode",
    )


def store(nexts, rows, after=()):
    parts, bins = nexts[0].shape[:2]
    n = len(nexts)

    def body(*refs):
        copies = []
        for c in range(n):
            for j in range(parts):
                to = refs[n].at[:, pl.ds(c * ROWS, ROWS), pl.ds(j * LANES, LANES)]
                copies.append(pltpu.make_async_copy(refs[c].at[j], to, refs[n + 2].at[c * parts + j]))
        for copy in copies:
            copy.start()
        refs[n + 1][...] = jnp.zeros(refs[n + 1].shape, F32)
        for copy in copies:
            copy.wait()

    size = bins * rows * parts * LANES
    return call(
        body,
        [(v, VMEM) for v in nexts],
        [((bins, rows, parts * LANES), F32, HBM), ((ROWS, LANES), F32)],
        (0, 8 * size),
        scratch=[pltpu.SemaphoreType.DMA((n * parts,))],
        after=after,
        name="store",
    )


def write_packed(ref, total):
    n = total.shape[0]
    most = jnp.max(jnp.max(jnp.abs(total), axis=1, keepdims=True), axis=0, keepdims=True)
    power = jnp.ceil(jnp.log2(jnp.maximum(most, 2.0**-100)))
    ref[0:n, :] = total
    ref[n:, :] = jnp.broadcast_to(power, (POWER_ROWS, total.shape[1]))


def write_scaled(refs, total, power):
    n, width = total.shape
    value = jnp.concatenate([total * jnp.exp2(-power), jnp.broadcast_to(power, (POWER_ROWS, width))], axis=0)
    write_columns(refs, 0, value)


def write_packed(refs, total):
    most = jnp.max(jnp.max(jnp.abs(total), axis=1, keepdims=True), axis=0, keepdims=True)
    power = jnp.ceil(jnp.log2(jnp.maximum(most, 2.0**-100)))
    write_scaled(refs, total, jnp.broadcast_to(power, (1, total.shape[1])))


def pack(total, cut, after=()):
    def body(total_ref, *out_refs):
        write_packed(out_refs, total_ref[...])

    n, width = total.shape
    outs = pieces_of((n + POWER_ROWS, width), F32, cut)
    return call(body, [(total, VMEM)], outs, (0, 0), after=after, name="pack")


def collect(spec, back, seed, cut=0, after=()):
    bins, cells = spec.shape
    hidden = back[0].shape[0]
    seeds = [seed] if seed is not None else []

    def body(spec_ref, *refs):
        values = read_columns(refs[: len(back)], 0, cells)
        total = lax.dot_general(spec_ref[...], values, (((1,), (1,)), ((), ())), preferred_element_type=F32)
        if seeds:
            total = total + refs[len(back)][...]
        if cut:
            write_packed(refs[len(back) + len(seeds) :], total)
        else:
            refs[-1][...] = total

    return call(
        body,
        [(v, VMEM) for v in (spec, *back, *seeds)],
        pieces_of((bins + POWER_ROWS, hidden), F32, cut) if cut else [((bins, hidden), F32)],
        (2 * bins * hidden * cells, 2 * bins * cells + 2 * hidden * cells),
        after=after,
        name="collect",
    )


def merge(mine, other, spare, after=()):
    rows, width = mine.shape
    n = rows - POWER_ROWS

    def body(mine_ref, other_ref, out_ref):
        here, there = mine_ref[n : n + 1], other_ref[n : n + 1]
        total = mine_ref[0:n] * jnp.exp2(here) + other_ref[0:n] * jnp.exp2(there)
        write_scaled([out_ref.at[0:rows]], total, jnp.maximum(here, there) + 1.0)
        if spare:
            out_ref[rows:] = jnp.zeros((spare, width), F32)

    values = [(mine, VMEM), (other, VMEM)]
    return call(body, values, [((rows + spare, width), F32)], (0, 0), after=after, name="merge")[0]


def merge_last(mine, other, n, after=()):
    k = len(mine)
    width = sum(v.shape[1] for v in mine)

    def body(*refs):
        out_ref, done_ref = refs[2 * k :]
        at = 0
        for a, b in zip(refs[:k], refs[k : 2 * k]):
            here, there = a[n : n + 1], b[n : n + 1]
            out_ref[:, at : at + a.shape[1]] = a[0:n] * jnp.exp2(here) + b[0:n] * jnp.exp2(there)
            at += a.shape[1]
        done_ref[...] = jnp.zeros(done_ref.shape, F32)

    values = [(v, VMEM) for v in (*mine, *other)]
    outs = [((n, width), F32, FREE), ((ROWS, LANES), F32)]
    return call(body, values, outs, (0, 0), after=after, name="merge_last")


def space_sum(packed, spare=0):
    n = packed[0].shape[0] - POWER_ROWS
    count = lax.axis_size("space")
    assert count & (count - 1) == 0 and count > 1
    bit = 1
    while True:
        mine = [lax.optimization_barrier(v.astype(F16)) for v in packed]
        other = [swap(v, "space", bit).astype(F32) for v in mine]
        mine = [v.astype(F32) for v in mine]
        bit *= 2
        after = yield packed[0]
        if bit >= count:
            yield merge_last(mine, other, n, after)
            return
        packed = [merge(a, b, spare if 2 * bit >= count else 0, after) for a, b in zip(mine, other)]


def courant(sectors, ndir, nfreq):
    angle = 2.0 * math.pi * (np.arange(NDIR) + 0.5) / NDIR
    speed = 1.0 / (1.0 + 2.3 * np.arange(nfreq) / nfreq)
    cx = np.abs(0.4 * np.cos(angle)[:, None] * speed[None, :])
    cy = np.abs(0.4 * np.sin(angle)[:, None] * speed[None, :])
    table = np.stack([1.0 - cx - cy - 0.3, cx, cy]).reshape(3, sectors, ndir * nfreq)
    return np.ascontiguousarray(table.transpose(1, 0, 2).reshape(3 * sectors, ndir * nfreq), np.float32)


def on_device(state, target, w_in, w_out, sea_mask, sea_count, turn_sign):
    ndir, nfreq, rows, lon = state.shape
    bins = ndir * nfreq
    hidden = w_in.shape[2]
    place = lax.axis_index("dir")
    sectors = lax.axis_size("dir")
    spaces = lax.axis_size("space")
    assert sectors == 4 and ndir * sectors == NDIR
    chunks, parts = rows // ROWS, lon // LANES
    place_ref = place.reshape(1)
    state = state.reshape(bins, rows, lon)
    target = target.reshape(bins, rows, lon)
    w_in = w_in.reshape(bins, hidden)
    w_out = jnp.transpose(w_out, (1, 2, 0)).reshape(bins, hidden)
    coef = jnp.asarray(courant(sectors, ndir, nfreq))

    tiles, far, spec, *send = encode_first(place_ref, state, sea_mask, w_in, ndir, 4)
    mask, w_in = send[-2:]
    near, send = send[4:-2], send[:4]
    pairs = []
    for s in range(spaces):
        for d in range(sectors):
            to = s - 1 if d >= sectors // 2 else s + 1
            if 0 <= to < spaces:
                pairs.append((s * sectors + d, to * sectors + d))
    far = swap(far.astype(F16), "dir", 3).astype(F32)

    def beside(values):
        return [swap(v.astype(F16), "dir", 1).astype(F32) for v in values]

    first = jnp.full((1, spec.shape[1]), PRE_SCALE, F32)
    tiles, near, specs, chips, crossed, stencils = [tiles], [beside(near)], [spec], [], [], []
    for c in range(chunks):
        if c > 0:
            spec, *send = encode(
                place_ref, tiles[c], mask, w_in, c, False, 4, after=[far, edge, stencils[0][0]] if c == 1 else after
            )
            specs.append(spec)
        received = [swap(v, "dir", 1) for v in send]
        spec, own = encode(place_ref, tiles[c], mask, w_in, c, True, after=[spec])
        specs.append(spec)
        chips.append(join([own], received, first, 1))
        crossed.append(cross(chips[c]))
        after = chips[c][:1]
        if c == 0:
            rest, more, edge = load_rest(place_ref, state, tiles[0], mask, ndir, after=after)
            tiles += rest
            near += [beside(v) for v in more]
            edge = lax.ppermute(edge.astype(F16), ("space", "dir"), pairs).astype(F32)
        stencils.append(
            stencil(
                place_ref, coef, tiles, near[c], far if c else None, edge, mask, turn_sign, sea_count, target,
                [w_out, turn_sign][c % 2], c, ndir, after=after,
            )
        )
    w_out = stencils[0][-1]
    after = [stencils[-1][0]]

    grad_out = None
    slopes, nexts, backs, back_crossed = [], [], [], []
    for c in range(chunks):
        base, goal, down, _, _ = stencils[c]
        if c == 0:
            base = turn_in(place_ref, coef, base, far, edge, mask, turn_sign, c, chunks, ndir, after=after)
        hid, slope = activate(chips[c], crossed[c], 4, after=[base, stencils[-1][0]] if c == 0 else after)
        slopes.append(slope)
        other = [swap(v, "dir", 1) for v in hid]
        own = []
        for mine, which in ((True, range(1)), (False, range(parts)), (True, range(1, parts))):
            base, grad_out, *out = decode(
                place_ref, hid if mine else other, w_out, base, goal, mask, sea_count, grad_out, c, mine, which,
                cut=len(which) if mine else 4,
            )
            if mine:
                own += out
            else:
                received = [swap(v, "dir", 1) for v in out]
        nexts.append(base)
        backs.append(join(own, received, down, 2 if c + 1 == chunks else 1))
        back_crossed.append(cross(backs[c]))
        after = backs[c][:1]

    out_sum = space_sum(pack(grad_out, 1), 112)
    next(out_sum)
    merged = out_sum.send(())
    next_state, stored = store(nexts, rows, after=[merged])

    grad_in = None
    after = []
    for c in range(chunks):
        last = c + 1 == chunks
        back = slope_back(
            backs[c], back_crossed[c], stencils[c][3], slopes[c], 4 if last else 2, after=after[:2]
        )
        (grad_in,) = collect(specs[2 * c + 1], back, grad_in)
        grad_in = collect(
            specs[2 * c], [swap(v, "dir", 1) for v in back], grad_in, cut=2 if last else 0
        )
        if c + 2 == chunks:
            (grad_in,) = grad_in
            waits = [stored]
            while not isinstance(merged, (tuple, list)):
                before, merged, waits = merged, out_sum.send(waits), ()
            grad_out, summed = merged
            after = [before, grad_in, summed]
        elif not last:
            (grad_in,) = grad_in

    in_sum = space_sum(grad_in)
    next(in_sum)
    merged = in_sum.send([summed])
    while not isinstance(merged, (tuple, list)):
        merged = in_sum.send(())
    grad_in = merged[0]
    return (
        next_state.reshape(ndir, nfreq, rows, lon),
        grad_in.reshape(ndir, nfreq, hidden),
        jnp.transpose(grad_out.reshape(ndir, nfreq, hidden), (2, 0, 1)),
    )


def solution(mesh):
    in_specs = (
        P("dir", None, "space", None),
        P("dir", None, "space", None),
        P("dir", None, None),
        P(None, "dir", None),
        P("space", None),
        P("space"),
        P("space", None),
    )
    out_specs = (P("dir", None, "space", None), P("dir", None, None), P(None, "dir", None))
    return jax.shard_map(
        on_device, mesh=mesh, in_specs=in_specs, out_specs=out_specs, check_vma=False
    )
```

```python
import math

import jax
import jax.numpy as jnp
import numpy as np
from jax import lax
from jax.experimental import pallas as pl
from jax.experimental.pallas import tpu as pltpu
from jax.sharding import PartitionSpec as P

NDIR = 36
ROWS = 8
LANES = 128
PRE_SCALE = 64.0
BACK_SCALE = 2.0**-8
LIMIT1 = 16
UNROLL = 32
POWER_ROWS = 16

BF16, F16, F32 = jnp.bfloat16, jnp.float16, jnp.float32
VMEM = pl.BlockSpec(memory_space=pltpu.VMEM)
SMEM = pl.BlockSpec(memory_space=pltpu.SMEM)
HBM = pl.BlockSpec(memory_space=pltpu.HBM)
ANY = pl.BlockSpec(memory_space=pl.ANY)
FREE = pl.BlockSpec(memory_space=pltpu.VMEM)


def swap(value, axis, bit):
    count = lax.axis_size(axis)
    return lax.ppermute(value, axis, [(i, i ^ bit) for i in range(count)])


def call(body, ins, outs, cost, after=(), aliases=None, scratch=(), limit=16, name=None):
    n = len(ins)

    def run(*refs):
        body(*refs[:n], *refs[n + len(after) :])

    def placed(dims, dtype, spec=VMEM):
        if spec is FREE:
            return jax.ShapeDtypeStruct(dims, dtype)
        return (pltpu.HBM if spec is HBM else pltpu.VMEM)(dims, dtype)

    values = [pltpu.with_memory_space_constraint(v, pltpu.HBM) if spec is HBM else v for v, spec in ins]
    return pl.pallas_call(
        run,
        in_specs=[spec for _, spec in ins] + [ANY] * len(after),
        out_specs=[VMEM if len(out) == 2 else out[2] for out in outs],
        out_shape=[placed(*out) for out in outs],
        scratch_shapes=list(scratch),
        input_output_aliases=aliases or {},
        compiler_params=pltpu.CompilerParams(vmem_limit_bytes=limit << 20),
        name=name,
    )(*values, *after)


def first_row(core, own):
    half = ROWS // 2
    return core * half if own else (1 - core) * half


def pick(ref, core, own, chunk, i, j):
    at = chunk * ROWS + i
    lanes = slice(j * LANES, (j + 1) * LANES)
    low, high = ref[at : at + 1, lanes], ref[at + ROWS // 2 : at + ROWS // 2 + 1, lanes]
    return jnp.where((core == 0) == own, low, high).astype(F32)


def count_of(count_ref, core, own, chunk, i):
    value = count_ref[chunk * ROWS + first_row(core, own) + i]
    return jnp.full((1, LANES), value, jnp.int32).astype(F32)


def write_columns(refs, start, value):
    offset = 0
    for ref in refs:
        for k in range(value.shape[1] // LANES):
            at = start + k * LANES - offset
            if 0 <= at < ref.shape[1]:
                ref[:, at : at + LANES] = value[:, k * LANES : (k + 1) * LANES]
        offset += ref.shape[1]


def read_columns(refs, start, width):
    found, offset = [], 0
    for ref in refs:
        low, high = max(start - offset, 0), min(start + width - offset, ref.shape[1])
        if low < high:
            found.append(ref[:, low:high])
        offset += ref.shape[1]
    return found[0] if len(found) == 1 else jnp.concatenate(found, axis=1)


def pieces_of(dims, dtype, cut):
    widths = cut if isinstance(cut, tuple) else (dims[1] // cut,) * cut
    return [((dims[0], width), dtype) for width in widths]


def encode_rows(place_ref, tiles_ref, mask_ref, w_ref, spec_ref, out_refs, chunk, own):
    parts, bins = tiles_ref.shape[:2]
    half = ROWS // 2
    wide = half * LANES
    core = place_ref[0] % 2
    first = first_row(core, own)
    for j in range(parts):
        flat = tiles_ref.at[j].reshape(bins * ROWS, LANES)
        cols = []
        for i in range(half):
            row = flat[pl.ds(first + i, bins, stride=ROWS), :]
            cols.append((row * pick(mask_ref, core, own, chunk, i, j)).astype(BF16))
        field = jnp.concatenate(cols, axis=1)
        spec_ref[:, j * wide : (j + 1) * wide] = field
        out = lax.dot_general(w_ref[...], field, (((0,), (0,)), ((), ())), preferred_element_type=F32)
        write_columns(out_refs, j * wide, out)


def block(ref, c, j, bins=slice(None)):
    return ref.at[bins, pl.ds(c * ROWS, ROWS), pl.ds(j * LANES, LANES)]


def copy_near(place, tiles_ref, near_refs, nfreq):
    start = pl.multiple_of((1 - place % 2) * (tiles_ref.shape[1] - nfreq), 8)
    for j, ref in enumerate(near_refs):
        ref[...] = tiles_ref[j, pl.ds(start, nfreq)]


def encode_first(place, state, mask, w_in, ndir, cut, after=()):
    bins, rows, lon = state.shape
    nfreq = bins // ndir
    hidden = w_in.shape[1]
    chunks, parts = rows // ROWS, lon // LANES
    cells = parts * ROWS * LANES // 2

    def body(place_ref, state_ref, mask_hbm, w_hbm, tiles_ref, far_ref, spec_ref, *refs):
        out_refs, near_refs, (mask_ref, w_ref, sems) = refs[:cut], refs[cut : cut + parts], refs[cut + parts :]
        place = place_ref[0]
        copies = [(block(state_ref, 0, j), tiles_ref.at[j]) for j in range(parts)]
        copies += [(mask_hbm, mask_ref), (w_hbm, w_ref)]
        edge = pl.ds(pl.multiple_of((place % 2) * (bins - nfreq), 8), nfreq)
        copies += [(block(state_ref, c, j, edge), far_ref.at[c, j]) for c in range(chunks) for j in range(parts)]
        copies = [pltpu.make_async_copy(*copy, sems.at[k]) for k, copy in enumerate(copies)]
        for copy in copies:
            copy.start()
        for copy in copies[: parts + 2]:
            copy.wait()
        encode_rows(place_ref, tiles_ref, mask_ref, w_ref, spec_ref, out_refs, 0, False)
        copy_near(place, tiles_ref, near_refs, nfreq)
        for copy in copies[parts + 2 :]:
            copy.wait()

    return call(
        body,
        [(place, SMEM), (state, HBM), (mask, HBM), (w_in, HBM)],
        [
            ((parts, bins, ROWS, LANES), F32),
            ((chunks, parts, nfreq, ROWS, LANES), F32),
            ((bins, cells), BF16),
            *pieces_of((hidden, cells), F32, cut),
            *[((nfreq, ROWS, LANES), F32)] * parts,
            (mask.shape, mask.dtype),
            (w_in.shape, w_in.dtype),
        ],
        (2 * bins * hidden * cells, 4 * bins * rows * lon),
        scratch=[pltpu.SemaphoreType.DMA(((1 + chunks) * parts + 2,))],
        after=after,
        name="encode_first",
    )


def load_rest(place, state, tiles, mask, ndir, after=()):
    bins, rows, lon = state.shape
    nfreq = bins // ndir
    chunks, parts = rows // ROWS, lon // LANES
    rest = chunks - 1

    def body(place_ref, state_ref, first_ref, mask_ref, *refs):
        tiles_refs, near_refs, (edge_ref, sems) = refs[:rest], refs[rest : rest + rest * parts], refs[rest + rest * parts :]
        copies = [
            pltpu.make_async_copy(block(state_ref, c + 1, j), tiles_refs[c].at[j], sems.at[c * parts + j])
            for c in range(rest)
            for j in range(parts)
        ]
        for copy in copies:
            copy.start()
        for copy in copies:
            copy.wait()
        for c in range(rest):
            copy_near(place_ref[0], tiles_refs[c], near_refs[c * parts : (c + 1) * parts], nfreq)
        for north in (False, True):
            at, i, ref = (0, 0, first_ref) if north else (rows - ROWS, ROWS - 1, tiles_refs[-1])

            @pl.when((place_ref[0] >= 2) == north)
            def _():
                for j in range(parts):
                    mask = mask_ref[at + i : at + i + 1, j * LANES : (j + 1) * LANES].astype(F32)
                    flat = ref.at[j].reshape(bins * ROWS, LANES)
                    edge_ref[j] = flat[pl.ds(i, bins, stride=ROWS), :] * mask

    outs = call(
        body,
        [(place, SMEM), (state, HBM), (tiles, VMEM), (mask, VMEM)],
        [(tiles.shape, F32)] * rest + [((nfreq, ROWS, LANES), F32)] * (rest * parts) + [((parts, bins, LANES), F32)],
        (0, 4 * bins * rows * lon),
        scratch=[pltpu.SemaphoreType.DMA((rest * parts,))],
        after=after,
        name="load_rest",
    )
    near = [outs[rest + c * parts : rest + (c + 1) * parts] for c in range(rest)]
    return outs[:rest], near, outs[-1]


def encode(place, tiles, mask, w_in, chunk, own, cut=1, after=()):
    parts, bins = tiles.shape[:2]
    hidden = w_in.shape[1]
    cells = parts * ROWS * LANES // 2

    def body(place_ref, tiles_ref, mask_ref, w_ref, spec_ref, *out_refs):
        encode_rows(place_ref, tiles_ref, mask_ref, w_ref, spec_ref, out_refs, chunk, own)

    return call(
        body,
        [(place, SMEM), (tiles, VMEM), (mask, VMEM), (w_in, VMEM)],
        [((bins, cells), BF16)] + pieces_of((hidden, cells), F32, cut),
        (2 * bins * hidden * cells, 4 * bins * cells),
        after=after,
        name="encode",
    )


def join(own, received, scale, cut, after=()):
    n, m = len(own), len(received)
    rows, width = own[0].shape[0], n * own[0].shape[1]

    def body(scale_ref, *refs):
        for k in range(width // LANES):
            at = slice(k * LANES, (k + 1) * LANES)
            total = read_columns(refs[:n], k * LANES, LANES) + read_columns(refs[n : n + m], k * LANES, LANES)
            write_columns(refs[n + m :], k * LANES, total * scale_ref[:, at])

    values = [(v, VMEM) for v in (scale, *own, *received)]
    return call(body, values, pieces_of((rows, width), F32, cut), (0, 0), after=after, name="join")


def cross(pieces):
    return [swap(v.astype(F16), "dir", 2).astype(F32) for v in pieces]


def activate(own, received, cut, after=()):
    n = len(own)
    rows, width = own[0].shape[0], n * own[0].shape[1]

    def body(*refs):
        own_refs, received_refs, slope_ref, hid_refs = refs[:n], refs[n : 2 * n], refs[2 * n], refs[2 * n + 1 :]
        for k in range(width // LANES):
            at = slice(k * LANES, (k + 1) * LANES)
            pre = read_columns(own_refs, k * LANES, LANES) + read_columns(received_refs, k * LANES, LANES)
            pre = pre * (1.0 / PRE_SCALE)
            sig = 1.0 / (1.0 + jnp.exp(-pre))
            slope_ref[:, at] = sig * (1.0 + pre * (1.0 - sig))
            write_columns(hid_refs, k * LANES, (pre * sig).astype(BF16))

    outs = [((rows, width), F32), *pieces_of((rows, width), BF16, cut)]
    slope, *hid = call(body, [(v, VMEM) for v in (*own, *received)], outs, (0, 0), after=after, name="activate")
    return hid, slope


def slope_back(own, received, up, slope, cut, after=()):
    n = len(own)

    def body(up_ref, slope_ref, *refs):
        for k in range(slope.shape[1] // LANES):
            at = slice(k * LANES, (k + 1) * LANES)
            total = read_columns(refs[:n], k * LANES, LANES) + read_columns(refs[n : 2 * n], k * LANES, LANES)
            write_columns(refs[2 * n :], k * LANES, (total * up_ref[:, at] * slope_ref[:, at]).astype(BF16))

    values = [(v, VMEM) for v in (up, slope, *own, *received)]
    return call(body, values, pieces_of(slope.shape, BF16, cut), (0, 0), after=after, name="slope_back")


def stencil(place, coef, tiles, near, far, edge, mask, sign, count, target, extra, chunk, ndir, after=()):
    chunks = len(tiles)
    parts, bins = tiles[chunk].shape[:2]
    nfreq = bins // ndir
    half = ROWS // 2
    wide = half * LANES
    around = {c: tiles[c] for c in range(max(chunk - 1, 0), min(chunk + 2, chunks))}
    others = [far, edge] if far is not None else []

    def body(place_ref, coef_ref, count_ref, target_ref, extra_ref, mask_ref, sign_ref, *refs):
        tiles_refs = dict(zip(around, refs))
        near_refs = refs[len(around) : len(around) + parts]
        other_refs = refs[len(around) + parts : len(around) + parts + len(others)]
        base_ref, goal_ref, down_ref, up_ref, kept_ref, sems = refs[len(around) + parts + len(others) :]
        copies = []
        for j in range(parts):
            copy = pltpu.make_async_copy(
                target_ref.at[:, pl.ds(chunk * ROWS, ROWS), pl.ds(j * LANES, LANES)], goal_ref.at[j], sems.at[j]
            )
            copy.start()
            copies.append(copy)
        copies.append(pltpu.make_async_copy(extra_ref, kept_ref, sems.at[parts]))
        copies[-1].start()
        place = place_ref[0]
        for i in range(half):
            counts = count_of(count_ref, place % 2, True, chunk, i)
            for j in range(parts):
                at = slice(j * wide + i * LANES, j * wide + (i + 1) * LANES)
                down_ref[:, at] = counts * BACK_SCALE
                up_ref[:, at] = (1.0 / BACK_SCALE) / counts
        lane = lax.broadcasted_iota(jnp.int32, (ROWS, LANES), 1)
        row = lax.broadcasted_iota(jnp.int32, (ROWS, LANES), 0)

        def plane(ref, c, j):
            return ref[c * ROWS : (c + 1) * ROWS, j * LANES : (j + 1) * LANES]

        masks = [[plane(mask_ref, c, j).astype(F32) for j in range(parts)] for c in range(chunks)]
        ahead = [plane(sign_ref, chunk, j) > 0 for j in range(parts)]

        def quadrant(q):
            east = q in (1, 2)
            north = q in (2, 3)
            beside = chunk + 1 if north else chunk - 1

            def sector(d, below, above):
                def group(g, _):
                    for u in range(UNROLL):
                        b, f = d * nfreq + g * UNROLL + u, g * UNROLL + u
                        here = [tiles_refs[chunk][j, b] for j in range(parts)]
                        field = [here[j] * masks[chunk][j] for j in range(parts)]
                        for j in range(parts):
                            k = j + 1 if east else j - 1
                            outer = field[k] if 0 <= k < parts else 0.0
                            if east:
                                x = pltpu.roll(jnp.where(lane == 0, outer, field[j]), LANES - 1, 1)
                            else:
                                x = pltpu.roll(jnp.where(lane == LANES - 1, outer, field[j]), 1, 1)
                            outer = 0.0
                            if 0 <= beside < chunks:
                                outer = tiles_refs[beside][j, b] * masks[beside][j]
                            if north:
                                y = pltpu.roll(jnp.where(row == 0, outer, field[j]), ROWS - 1, 0)
                            else:
                                y = pltpu.roll(jnp.where(row == ROWS - 1, outer, field[j]), 1, 0)
                            upstream = jnp.where(ahead[j], below(b, f, j), above(b, f, j))
                            total = coef_ref[3 * q, b] * here[j] + coef_ref[3 * q + 1, b] * x
                            total = total + (coef_ref[3 * q + 2, b] * y + 0.3 * upstream)
                            base_ref[j, b] = total * masks[chunk][j]
                    return 0

                lax.fori_loop(0, nfreq // UNROLL, group, 0)

            def far_bin(b, f, j):
                return other_refs[0][chunk, j, f] if others else jnp.zeros((ROWS, LANES), F32)

            def near_bin(b, f, j):
                return near_refs[j][f]

            def inside(shift):
                return lambda b, f, j: tiles_refs[chunk][j, b + shift]

            sector(0, near_bin if q % 2 else far_bin, inside(nfreq))

            def middle(d, _):
                sector(d, inside(-nfreq), inside(nfreq))
                return 0

            lax.fori_loop(1, ndir - 1, middle, 0)
            sector(ndir - 1, inside(-nfreq), far_bin if q % 2 else near_bin)

        for q in range(4):
            pl.when(place == q)(lambda q=q: quadrant(q))
        if others:
            blow_in(place, coef_ref, other_refs[1], mask_ref, base_ref, chunk, chunks, ndir)
        for copy in copies:
            copy.wait()
        if far is not None:
            subtract(base_ref, goal_ref, goal_ref, nfreq)

    cells = parts * ROWS * LANES
    return call(
        body,
        [(place, SMEM), (coef, SMEM), (count, SMEM), (target, HBM), (extra, HBM)]
        + [(v, VMEM) for v in (mask, sign, *around.values(), *near, *others)],
        [
            ((parts, bins, ROWS, LANES), F32),
            ((parts, bins, ROWS, LANES), F32),
            ((1, cells // 2), F32),
            ((1, cells // 2), F32),
            (extra.shape, extra.dtype),
        ],
        (40 * bins * cells, 8 * bins * cells),
        scratch=[pltpu.SemaphoreType.DMA((parts + 1,))],
        after=after,
        limit=32,
        name="stencil",
    )


def blow_in(place, coef_ref, edge_ref, mask_ref, base_ref, chunk, chunks, ndir):
    parts, bins = base_ref.shape[:2]
    nfreq = bins // ndir
    freq = lax.broadcasted_iota(jnp.int32, (nfreq, LANES), 0).astype(F32)
    speed = 1.0 / (1.0 + 2.3 * freq / nfreq)

    def blow(i):
        for j in range(parts):
            flat = base_ref.at[j].reshape(bins * ROWS, LANES)
            mask = mask_ref[chunk * ROWS + i : chunk * ROWS + i + 1, j * LANES : (j + 1) * LANES].astype(F32)
            for d in range(ndir):
                at = pl.ds(d * nfreq * ROWS + i, nfreq, stride=ROWS)
                cy = coef_ref[3 * place + 2, d * nfreq] * speed
                flat[at, :] = flat[at, :] + (mask * cy) * edge_ref[j, d * nfreq : (d + 1) * nfreq, :]

    if chunk == 0:
        pl.when(place < 2)(lambda: blow(0))
    if chunk == chunks - 1:
        pl.when(place >= 2)(lambda: blow(ROWS - 1))


def subtract(base_ref, goal_ref, out_ref, nfreq):
    parts, bins = base_ref.shape[:2]

    def group(g, _):
        at = pl.ds(g * nfreq, nfreq)
        for j in range(parts):
            out_ref[j, at] = base_ref[j, at] - goal_ref[j, at]
        return 0

    lax.fori_loop(0, bins // nfreq, group, 0)


def turn_in(place, coef, base, goal, far, edge, mask, sign, chunk, chunks, ndir, after=()):
    parts, bins = base.shape[:2]
    nfreq = bins // ndir

    def body(place_ref, coef_ref, base_ref, goal_ref, far_ref, edge_ref, mask_ref, sign_ref, out_ref, less_ref):
        place = place_ref[0]
        upper = place % 2
        start = pl.multiple_of(upper * (bins - nfreq), 8)
        for j in range(parts):
            at = (slice(chunk * ROWS, (chunk + 1) * ROWS), slice(j * LANES, (j + 1) * LANES))
            ahead = jnp.where(sign_ref[at] > 0, 1, 0)
            share = jnp.where(ahead != upper, 0.3 * mask_ref[at].astype(F32), 0.0)
            bin_edge = pl.ds(start, nfreq)
            out_ref[j, bin_edge] = base_ref[j, bin_edge] + share[None] * far_ref[chunk, j]
        blow_in(place, coef_ref, edge_ref, mask_ref, out_ref, chunk, chunks, ndir)

        subtract(out_ref, goal_ref, less_ref, nfreq)

    ins = [(place, SMEM), (coef, SMEM)] + [(v, VMEM) for v in (base, goal, far, edge, mask, sign)]
    outs = [(base.shape, F32), (base.shape, F32)]
    return call(body, ins, outs, (0, 0), after=after, aliases={2: 0, 3: 1}, name="turn_in")


def decode(place, hid, w_out, less, mask, count, seed, chunk, own, which, cut=1, after=()):
    bins = less.shape[1]
    hidden = w_out.shape[1]
    half = ROWS // 2
    wide = half * LANES
    cells = len(which) * wide
    seeds = [seed] if seed is not None else []

    def body(place_ref, count_ref, w_ref, less_ref, mask_ref, *refs):
        hid_refs, refs = refs[: len(hid)], refs[len(hid) :]
        next_ref, grad_ref, *out_refs, back_ref = refs[len(seeds) :]
        core = place_ref[0] % 2
        first = first_row(core, own)
        total = refs[0][...] if seeds else jnp.zeros(grad_ref.shape, F32)
        for k, j in enumerate(which):
            rest = less_ref.at[j].reshape(bins * ROWS, LANES)
            units = read_columns(hid_refs, j * wide, wide)
            source = jnp.dot(w_ref[...], units, preferred_element_type=F32)
            for i in range(half):
                at = pl.ds(first + i, bins, stride=ROWS)
                mask = pick(mask_ref, core, own, chunk, i, j)
                weight = (1.0 / count_of(count_ref, core, own, chunk, i)) * mask
                part = source[:, i * LANES : (i + 1) * LANES]
                new = (0.5 * mask) * part
                next_ref[:, k * wide + i * LANES : k * wide + (i + 1) * LANES] = new
                back_ref[:, i * LANES : (i + 1) * LANES] = (weight * (rest[at, :] + new)).astype(BF16)
            back = back_ref[...]
            total = total + lax.dot_general(back, units, (((1,), (1,)), ((), ())), preferred_element_type=F32)
            out = lax.dot_general(w_ref[...], back, (((0,), (0,)), ((), ())), preferred_element_type=F32)
            write_columns(out_refs, k * wide, out)
        grad_ref[...] = total

    return call(
        body,
        [(place, SMEM), (count, SMEM)] + [(v, VMEM) for v in (w_out, less, mask, *hid, *seeds)],
        [((bins, cells), F32), ((bins, hidden), F32)] + pieces_of((hidden, cells), F32, cut),
        (6 * bins * hidden * cells, 12 * bins * cells),
        scratch=[pltpu.VMEM((bins, wide), BF16)],
        after=after,
        name="decode",
    )


def store(place, base, own, other, chunk, rows, before=None, after=()):
    bins = other.shape[0]
    half = ROWS // 2
    parts = other.shape[1] // (half * LANES)
    n = len(own)
    held = [before] if before is not None else []

    def body(place_ref, base_ref, other_ref, *refs):
        own_refs, (out_ref, done_ref, tiles_ref, sems) = refs[:n], refs[n + len(held) :]
        core = place_ref[0] % 2
        copies = []
        for j in range(parts):
            flat = tiles_ref.at[j].reshape(bins * ROWS, LANES)
            base = base_ref.at[j].reshape(bins * ROWS, LANES)
            for mine, values in ((True, own_refs), (False, [other_ref])):
                for i in range(half):
                    at = pl.ds(first_row(core, mine) + i, bins, stride=ROWS)
                    flat[at, :] = base[at, :] + read_columns(values, (j * half + i) * LANES, LANES)
            copies.append(pltpu.make_async_copy(tiles_ref.at[j], block(out_ref, chunk, j), sems.at[j]))
            copies[j].start()
        done_ref[...] = jnp.zeros(done_ref.shape, F32)
        for copy in copies:
            copy.wait()

    return call(
        body,
        [(place, SMEM), (base, VMEM), (other, VMEM)] + [(v, VMEM) for v in own] + [(v, HBM) for v in held],
        [((bins, rows, parts * LANES), F32, HBM), ((ROWS, LANES), F32)],
        (0, 0),
        scratch=[pltpu.VMEM((parts, bins, ROWS, LANES), F32), pltpu.SemaphoreType.DMA((parts,))],
        aliases={3 + n: 0} if held else None,
        after=after,
        name="store",
    )


def write_scaled(refs, total, power):
    n, width = total.shape
    value = jnp.concatenate([total * jnp.exp2(-power), jnp.broadcast_to(power, (POWER_ROWS, width))], axis=0)
    write_columns(refs, 0, value)


def write_packed(refs, total):
    most = jnp.max(jnp.max(jnp.abs(total), axis=1, keepdims=True), axis=0, keepdims=True)
    power = jnp.ceil(jnp.log2(jnp.maximum(most, 2.0**-100)))
    write_scaled(refs, total, jnp.broadcast_to(power, (1, total.shape[1])))


def pack(total, cut, after=()):
    def body(total_ref, *out_refs):
        write_packed(out_refs, total_ref[...])

    n, width = total.shape
    outs = pieces_of((n + POWER_ROWS, width), F32, cut)
    return call(body, [(total, VMEM)], outs, (0, 0), after=after, name="pack")


def collect(spec, back, seed, cut=0, after=()):
    bins, cells = spec.shape
    hidden = back[0].shape[0]
    seeds = [seed] if seed is not None else []

    def body(spec_ref, *refs):
        values = read_columns(refs[: len(back)], 0, cells)
        total = lax.dot_general(spec_ref[...], values, (((1,), (1,)), ((), ())), preferred_element_type=F32)
        if seeds:
            total = total + refs[len(back)][...]
        if cut:
            write_packed(refs[len(back) + len(seeds) :], total)
        else:
            refs[-1][...] = total

    return call(
        body,
        [(v, VMEM) for v in (spec, *back, *seeds)],
        pieces_of((bins + POWER_ROWS, hidden), F32, cut) if cut else [((bins, hidden), F32)],
        (2 * bins * hidden * cells, 2 * bins * cells + 2 * hidden * cells),
        after=after,
        name="collect",
    )


def merge(mine, other, spare, after=()):
    rows, width = mine.shape
    n = rows - POWER_ROWS

    def body(mine_ref, other_ref, out_ref):
        here, there = mine_ref[n : n + 1], other_ref[n : n + 1]
        total = mine_ref[0:n] * jnp.exp2(here) + other_ref[0:n] * jnp.exp2(there)
        write_scaled([out_ref.at[0:rows]], total, jnp.maximum(here, there) + 1.0)
        if spare:
            out_ref[rows:] = jnp.zeros((spare, width), F32)

    values = [(mine, VMEM), (other, VMEM)]
    return call(body, values, [((rows + spare, width), F32)], (0, 0), after=after, name="merge")[0]


def merge_last(mine, other, n, after=()):
    k = len(mine)
    width = sum(v.shape[1] for v in mine)

    def body(*refs):
        out_ref, done_ref = refs[2 * k :]
        at = 0
        for a, b in zip(refs[:k], refs[k : 2 * k]):
            here, there = a[n : n + 1], b[n : n + 1]
            out_ref[:, at : at + a.shape[1]] = a[0:n] * jnp.exp2(here) + b[0:n] * jnp.exp2(there)
            at += a.shape[1]
        done_ref[...] = jnp.zeros(done_ref.shape, F32)

    values = [(v, VMEM) for v in (*mine, *other)]
    outs = [((n, width), F32, FREE), ((ROWS, LANES), F32)]
    return call(body, values, outs, (0, 0), after=after, name="merge_last")


def space_sum(packed, spare=0):
    n = packed[0].shape[0] - POWER_ROWS
    count = lax.axis_size("space")
    assert count & (count - 1) == 0 and count > 1
    bit = 1
    while True:
        mine = [lax.optimization_barrier(v.astype(F16)) for v in packed]
        other = [swap(v, "space", bit).astype(F32) for v in mine]
        mine = [v.astype(F32) for v in mine]
        bit *= 2
        after = yield packed[0]
        if bit >= count:
            yield merge_last(mine, other, n, after)
            return
        packed = [merge(a, b, spare if 2 * bit >= count else 0, after) for a, b in zip(mine, other)]


def courant(sectors, ndir, nfreq):
    angle = 2.0 * math.pi * (np.arange(NDIR) + 0.5) / NDIR
    speed = 1.0 / (1.0 + 2.3 * np.arange(nfreq) / nfreq)
    cx = np.abs(0.4 * np.cos(angle)[:, None] * speed[None, :])
    cy = np.abs(0.4 * np.sin(angle)[:, None] * speed[None, :])
    table = np.stack([1.0 - cx - cy - 0.3, cx, cy]).reshape(3, sectors, ndir * nfreq)
    return np.ascontiguousarray(table.transpose(1, 0, 2).reshape(3 * sectors, ndir * nfreq), np.float32)


def on_device(state, target, w_in, w_out, sea_mask, sea_count, turn_sign):
    ndir, nfreq, rows, lon = state.shape
    bins = ndir * nfreq
    hidden = w_in.shape[2]
    place = lax.axis_index("dir")
    sectors = lax.axis_size("dir")
    spaces = lax.axis_size("space")
    assert sectors == 4 and ndir * sectors == NDIR
    chunks, parts = rows // ROWS, lon // LANES
    place_ref = place.reshape(1)
    state = state.reshape(bins, rows, lon)
    target = target.reshape(bins, rows, lon)
    w_in = w_in.reshape(bins, hidden)
    w_out = jnp.transpose(w_out, (1, 2, 0)).reshape(bins, hidden)
    coef = jnp.asarray(courant(sectors, ndir, nfreq))

    tiles, far, spec, *send = encode_first(place_ref, state, sea_mask, w_in, ndir, 4)
    mask, w_in = send[-2:]
    near, send = send[4:-2], send[:4]
    pairs = []
    for s in range(spaces):
        for d in range(sectors):
            to = s - 1 if d >= sectors // 2 else s + 1
            if 0 <= to < spaces:
                pairs.append((s * sectors + d, to * sectors + d))
    far = swap(far.astype(F16), "dir", 3).astype(F32)

    def beside(values):
        return [swap(v.astype(F16), "dir", 1).astype(F32) for v in values]

    first = jnp.full((1, spec.shape[1]), PRE_SCALE, F32)
    tiles, near, specs, chips, crossed, stencils = [tiles], [beside(near)], [spec], [], [], []
    for c in range(chunks):
        if c > 0:
            spec, *send = encode(
                place_ref, tiles[c], mask, w_in, c, False, 4, after=[far, edge, stencils[0][0]] if c == 1 else after
            )
            specs.append(spec)
        received = [swap(v, "dir", 1) for v in send]
        spec, own = encode(place_ref, tiles[c], mask, w_in, c, True, after=[spec])
        specs.append(spec)
        chips.append(join([own], received, first, 1))
        crossed.append(cross(chips[c]))
        after = chips[c][:1]
        if c == 0:
            rest, more, edge = load_rest(place_ref, state, tiles[0], mask, ndir, after=after)
            tiles += rest
            near += [beside(v) for v in more]
            edge = lax.ppermute(edge.astype(F16), ("space", "dir"), pairs).astype(F32)
            stencils = [
                stencil(
                    place_ref, coef, tiles, near[0], None, edge, mask, turn_sign, sea_count, target, w_out, 0, ndir,
                    after=after,
                )
            ]
    w_out = stencils[0][-1]
    after = [*chips[-1], *[v for values in near[1:] for v in values]]

    grad_out = None
    slopes, nexts, backs, back_crossed = [], [], [], []
    for c in range(chunks):
        if c > 0:
            stencils.append(
                stencil(
                    place_ref, coef, tiles, near[c], far, edge, mask, turn_sign, sea_count, target, turn_sign, c,
                    ndir, after=after,
                )
            )
            after = stencils[c][:1]
        base, goal, down, _, _ = stencils[c]
        if c == 0:
            base, goal = turn_in(place_ref, coef, base, goal, far, edge, mask, turn_sign, c, chunks, ndir, after=after)
        hid, slope = activate(chips[c], crossed[c], 4, after=[base, goal] if c == 0 else after)
        slopes.append(slope)
        other = [swap(v, "dir", 1) for v in hid]
        own, own_new = [], []
        for mine, which in ((True, range(1)), (False, range(parts)), (True, range(1, parts))):
            new, grad_out, *out = decode(
                place_ref, hid if mine else other, w_out, goal, mask, sea_count, grad_out, c, mine, which,
                cut=len(which) if mine else 4,
            )
            if mine:
                own += out
                own_new.append(new)
            else:
                received = [swap(v, "dir", 1) for v in out]
                other_new = new
        nexts.append((base, own_new, other_new))
        backs.append(join(own, received, down, 2 if c + 1 == chunks else 1))
        back_crossed.append(cross(backs[c]))
        after = backs[c][:1]

    out_sum = space_sum(pack(grad_out, 1), 112)
    next(out_sum)
    merged = out_sum.send(())
    next_state, stored = store(place_ref, *nexts[0], 0, rows, after=[merged])

    grad_in = None
    after = []
    for c in range(chunks):
        last = c + 1 == chunks
        back = slope_back(
            backs[c], back_crossed[c], stencils[c][3], slopes[c], 4 if last else 2, after=after[:2]
        )
        (grad_in,) = collect(specs[2 * c + 1], back, grad_in)
        grad_in = collect(
            specs[2 * c], [swap(v, "dir", 1) for v in back], grad_in, cut=2 if last else 0
        )
        if c + 2 == chunks:
            (grad_in,) = grad_in
            waits = [stored]
            while not isinstance(merged, (tuple, list)):
                before, merged, waits = merged, out_sum.send(waits), ()
            grad_out, summed = merged
            after = [before, grad_in, summed]
        elif not last:
            (grad_in,) = grad_in

    in_sum = space_sum(grad_in)
    next(in_sum)
    merged = in_sum.send([summed])
    for c in range(1, chunks):
        next_state, stored = store(place_ref, *nexts[c], c, rows, next_state, after=[merged])
    waits = [stored]
    while not isinstance(merged, (tuple, list)):
        merged, waits = in_sum.send(waits), ()
    grad_in = merged[0]
    return (
        next_state.reshape(ndir, nfreq, rows, lon),
        grad_in.reshape(ndir, nfreq, hidden),
        jnp.transpose(grad_out.reshape(ndir, nfreq, hidden), (2, 0, 1)),
    )


def solution(mesh):
    in_specs = (
        P("dir", None, "space", None),
        P("dir", None, "space", None),
        P("dir", None, None),
        P(None, "dir", None),
        P("space", None),
        P("space"),
        P("space", None),
    )
    out_specs = (P("dir", None, "space", None), P("dir", None, None), P(None, "dir", None))
    return jax.shard_map(
        on_device, mesh=mesh, in_specs=in_specs, out_specs=out_specs, check_vma=False
    )
```
